256 devices in a mesh: row: 8 (over x_lo, y), col: 32 (over z, x_hi, core).
Axes of the slice: x: 4 (x_hi: 2, x_lo: 2; x = x_hi * 2 + x_lo), y: 4, z: 8, core: 2. Of those that a mesh axis runs over, the one named last changes fastest.
Arguments:
- latent: bfloat16 [512, 1024, 320], P('row', 'col')
- stale_input: bfloat16 [512, 1024, 320], P('row', 'col')
- stale_hidden: bfloat16 [512, 1024, 320], P('row', 'col')
- refresh: int32 [64, 32], P('row', 'col'), may hold values from 0 to 1, as said below
- gain_one: float32 [320], replicated, may hold values from 0.1 to 1.9
- weight_one: bfloat16 [9, 320, 320], replicated, may hold values from -0.109375 to 0.109375
- time_shift: float32 [320], replicated, may hold values from -4 to 4
- gain_two: float32 [320], replicated, may hold values from 0.1 to 1.9
- weight_two: bfloat16 [9, 320, 320], replicated, may hold values from -0.109375 to 0.109375
Outputs:
- block_out: bfloat16 [512, 1024, 320], P('row', 'col')
- fresh_hidden: bfloat16 [512, 1024, 320], P('row', 'col')
The draws below stay inside these ranges and needn't reach their ends.
Inputs may be any that keep to these rules, and one draw needn't show every extreme that they name: refresh[k, c] is 1 where strip k (rows k * 8 onward) of tile column c is recomputed. The tiles of tile columns c and c plus half the number of tile columns, in the same tile row, hold at most 8 such strips together. In every draw the tile of the first tile row in the middle tile column and the tile of the last tile row in the last tile column hold all 8, and their paired tiles none.
All inputs are finite; a program needn't handle non-finite values.
Results may differ from the reference program's by a relative error of at most 0.0035.
Values may be sent and summed in bfloat16 or wider, within the bound.
A program may use at most 128 MiB of HBM per device.

```python
import math
import jax
import jax.numpy as jnp
from jax import lax

C = 320
GROUPS = 32
TH = 64
TW = 32
SH = 8
STRIPS = 8
GRID_ROWS = 512
GRID_COLS = 1024
N_ROW = 8
N_COL = 32


def scale_field(key):
    channel_scale = jnp.exp(jax.random.uniform(jax.random.fold_in(key, 11), (C,), jnp.float32, math.log(0.3), math.log(3.0)))
    row_tiles = jnp.exp(jax.random.uniform(jax.random.fold_in(key, 12), (N_ROW,), jnp.float32, -math.log(1.5), math.log(1.5)))
    col_tiles = jnp.exp(jax.random.uniform(jax.random.fold_in(key, 13), (N_COL,), jnp.float32, -math.log(2.5), math.log(2.5)))
    downward = jnp.repeat(row_tiles, TH)
    sideways = jnp.repeat(col_tiles, TW)
    grid_scale = downward[:, None] * sideways[None, :]
    return grid_scale[:, :, None] * channel_scale


def noisy(key, row_spread):
    shape = (TH * N_ROW, TW * N_COL, C)
    noise = jax.random.normal(key, shape, jnp.float32)
    row_factor = jnp.exp(jax.random.uniform(jax.random.fold_in(key, 5), (TH * N_ROW, 1, 1), jnp.float32, 0.0, math.log(row_spread)))
    return noise * row_factor


def draw_latent(key, part):
    scales = scale_field(key)
    key = jax.random.fold_in(key, 1)
    own_channels = jnp.exp(jax.random.uniform(jax.random.fold_in(key, 21), (C,), jnp.float32, math.log(0.5), math.log(2.0)))
    values = noisy(key, 1.0)
    return (values * scales * own_channels).astype(jnp.bfloat16)


def draw_stale_input(key, part):
    scales = scale_field(key)
    key = jax.random.fold_in(key, 2)
    values = noisy(key, 1.0)
    return (values * scales).astype(jnp.bfloat16)


def draw_stale_hidden(key, part):
    key = jax.random.fold_in(key, 3)
    scales = scale_field(key)
    values = noisy(key, 1.0)
    return (values * scales).astype(jnp.bfloat16)


def draw_refresh(key, part):
    key = jax.random.fold_in(key, 4)
    keys = jax.random.split(key, 5)
    half = N_COL // 2
    first = jax.random.randint(keys[0], (N_ROW, half), 0, STRIPS + 1)
    second = jax.random.randint(keys[1], (N_ROW, half), 0, STRIPS - first + 1)
    pair_ids = jnp.arange(N_ROW * half, dtype=jnp.int32).reshape(N_ROW, half)
    forced = jnp.logical_or(pair_ids == 0, pair_ids == N_ROW * half - 1)
    first = jnp.where(forced, STRIPS, first)
    second = jnp.where(forced, 0, second)
    flipped = jax.random.randint(keys[3], (N_ROW, half), 0, 2)
    flipped = jnp.where(forced, 1, flipped)
    left = jnp.where(flipped == 1, second, first)
    right = jnp.where(flipped == 1, first, second)
    counts = jnp.concatenate([left, right], axis=1)
    offsets = jax.random.randint(keys[4], (N_ROW, N_COL), 0, STRIPS)
    position = jnp.arange(STRIPS, dtype=jnp.int32)
    live = (position[None, :, None] - offsets[:, None, :]) % STRIPS < counts[:, None, :]
    return live.astype(jnp.int32).reshape(N_ROW * STRIPS, N_COL)


def gaussian(rng, extent, deviation, most, kind=jnp.bfloat16):
    return jnp.clip(deviation * jax.random.normal(rng, extent, jnp.float32), -most, most).astype(kind)


def setup_inputs(seed: int = 0) -> dict:
    arg_keys = jax.random.split(jax.random.key(seed), 10)
    return {
        "latent": draw_latent(jax.random.fold_in(arg_keys[9], 71), 0),
        "stale_input": draw_stale_input(jax.random.fold_in(arg_keys[9], 71), 0),
        "stale_hidden": draw_stale_hidden(jax.random.fold_in(arg_keys[9], 71), 0),
        "refresh": draw_refresh(jax.random.fold_in(arg_keys[9], 71), 0),
        "gain_one": jnp.clip(1.0 + 0.18 * jax.random.normal(arg_keys[4], (C,), jnp.float32), 0.1, 1.9),
        "weight_one": gaussian(arg_keys[5], (9, C, C), (9 * C) ** -0.5, 0.109375),
        "time_shift": gaussian(arg_keys[6], (C,), 1.0, 4.0, jnp.float32),
        "gain_two": jnp.clip(1.0 + 0.18 * jax.random.normal(arg_keys[7], (C,), jnp.float32), 0.1, 1.9),
        "weight_two": gaussian(arg_keys[8], (9, C, C), (9 * C) ** -0.5, 0.109375),
    }


EPSILON = 1e-05

def group_stats(values):
    grouped = values.astype(jnp.float32).reshape(-1, GROUPS, C // GROUPS)
    cell_count = float(GRID_ROWS * GRID_COLS * (C // GROUPS))
    center = lax.optimization_barrier(jnp.sum(grouped, axis=(0, 2))) / cell_count
    spread = lax.rsqrt(lax.optimization_barrier(jnp.sum(grouped * grouped, axis=(0, 2))) / cell_count - center * center + EPSILON)
    return (center, spread)

def activate(values, center, spread, scaling):
    grouped = values.astype(jnp.float32).reshape(values.shape[:-1] + (GROUPS, C // GROUPS))
    scaled = ((grouped - center[:, None]) * spread[:, None]).reshape(values.shape)
    return jax.nn.silu(scaled * scaling).astype(jnp.bfloat16)

def reference(latent, stale_input, stale_hidden, refresh, gain_one, weight_one, time_shift, gain_two, weight_two):
    center_in, spread_in = group_stats(stale_input)
    center_hid, spread_hid = group_stats(stale_hidden)
    current = activate(latent, center_in, spread_in, gain_one)
    stale_first = activate(stale_input, center_in, spread_in, gain_one)
    stale_second = activate(stale_hidden, center_hid, spread_hid, gain_two)
    margins = ((1, 1), (1, 1), (0, 0))
    padded_current = jnp.pad(current, margins)
    padded_first = jnp.pad(stale_first, margins)
    padded_second = jnp.pad(stale_second, margins)
    columns = jnp.arange(GRID_COLS, dtype=jnp.int32)
    strip_rows = jnp.arange(SH, dtype=jnp.int32)

    def mixed_conv(fresh_padded, stale_padded, weight):
        summed = jnp.zeros((SH * GRID_COLS, C), jnp.float32)
        for tap_index in range(9):
            shift_row, shift_col = divmod(tap_index, 3)
            row_inside = jnp.logical_and(strip_rows + shift_row - 1 >= 0, strip_rows + shift_row - 1 < SH)
            col_inside = (columns + shift_col - 1) // TW == columns // TW
            same_strip = jnp.logical_and(row_inside[:, None], col_inside[None, :])[:, :, None]
            fresh_tap = fresh_padded[shift_row:shift_row + SH, shift_col:shift_col + GRID_COLS]
            stale_tap = stale_padded[shift_row:shift_row + SH, shift_col:shift_col + GRID_COLS]
            tap_values = jnp.where(same_strip, fresh_tap, stale_tap)
            summed = summed + jnp.dot(tap_values.reshape(-1, C), weight[tap_index], preferred_element_type=jnp.float32)
        return summed.reshape(SH, GRID_COLS, C)

    def one_band(band_index):
        first_row = band_index * SH
        fresh_one = lax.dynamic_slice_in_dim(padded_current, first_row, SH + 2, 0)
        stale_one = lax.dynamic_slice_in_dim(padded_first, first_row, SH + 2, 0)
        hidden_new = (mixed_conv(fresh_one, stale_one, weight_one) + time_shift).astype(jnp.bfloat16)
        second = activate(hidden_new, center_hid, spread_hid, gain_two)
        fresh_two = jnp.pad(second, margins)
        stale_two = lax.dynamic_slice_in_dim(padded_second, first_row, SH + 2, 0)
        base_rows = lax.dynamic_slice_in_dim(latent, first_row, SH, 0)
        finished = (base_rows.astype(jnp.float32) + mixed_conv(fresh_two, stale_two, weight_two)).astype(jnp.bfloat16)
        flags = jnp.take(refresh[band_index], columns // TW) > 0
        chosen = flags[None, :, None]
        old_hidden = lax.dynamic_slice_in_dim(stale_hidden, first_row, SH, 0)
        return (jnp.where(chosen, finished, base_rows), jnp.where(chosen, hidden_new, old_hidden))
    block_bands, hidden_bands = lax.map(one_band, jnp.arange(GRID_ROWS // SH, dtype=jnp.int32))
    return (block_bands.reshape(GRID_ROWS, GRID_COLS, C), hidden_bands.reshape(GRID_ROWS, GRID_COLS, C))
```

```python
import functools

import jax
import jax.numpy as jnp
from jax import lax
from jax.experimental import pallas as pl
from jax.experimental.pallas import tpu as pltpu
from jax.sharding import PartitionSpec as P

GROUPS = 32
SH = 8
EPSILON = 1e-05
LANES = 128
EXACT = lax.Precision.HIGHEST
F32 = jnp.float32
BF16 = jnp.bfloat16


def act(values, center, half_scale):
    half = (values - center) * half_scale
    return half * jnp.tanh(half) + half


def one_hot(condition, kind=F32):
    return jnp.where(condition, 1.0, 0.0).astype(kind)


def total_wait(buffer, semaphore):
    pltpu.make_async_copy(buffer, buffer, semaphore).wait()


def margins_kernel(
    cell_count,
    shape,
    stale_in,
    stale_hid,
    gain_one,
    gain_two,
    stats_out,
    rows_out,
    cols_out,
    tiles,
    cols,
    rows_in,
    cols_in,
    corners_in,
    part,
    part_in,
    group,
    group_in,
    load_sem,
    side_send,
    side_recv,
    sum_send,
    sum_recv,
):
    n_row, n_col = shape
    row, col = lax.axis_index("row"), lax.axis_index("col")
    tile_rows, tile_cols, channels = tiles.shape[1:]
    strips = tile_rows // SH
    up, down = lax.rem(row + n_row - 1, n_row), lax.rem(row + 1, n_row)
    left, right = lax.rem(col + n_col - 1, n_col), lax.rem(col + 1, n_col)
    core, site = lax.rem(col, 2), lax.div(col, 2)
    sites = n_col // 2
    first_peers, second_peers = 2 * n_row - 1, sites - 1

    def first_peer(step):
        place = lax.rem(row * 2 + core + step, 2 * n_row)
        return lax.div(place, 2), site * 2 + lax.rem(place, 2)

    def second_peer(step):
        return row, lax.rem(site + step, sites) * 2 + core

    def signal(device):
        pl.semaphore_signal(
            barrier, inc=1, device_id=device, device_id_type=pl.DeviceIdType.MESH
        )

    loads = []
    half = tile_rows // 2
    for index, source in enumerate((stale_in, stale_hid)):
        for piece in range(2):
            span = pl.ds(piece * half, half)
            copy = pltpu.make_async_copy(
                source.at[span], tiles.at[index, span], load_sem.at[index, piece]
            )
            copy.start()
            loads.append(copy)

    barrier = pltpu.get_barrier_semaphore()

    @pl.loop(1, first_peers + 1)
    def _(step):
        signal(first_peer(step))

    @pl.loop(1, second_peers + 1)
    def _(step):
        signal(second_peer(step))

    for device in ((up, left), (up, right), (row, left), (row, right), (down, left), (down, right)):
        signal(device)

    lines = lax.broadcasted_iota(jnp.int32, (channels, LANES), 0)
    lanes = lax.rem(lax.broadcasted_iota(jnp.int32, (channels, LANES), 1), GROUPS)
    size = channels // GROUPS
    gather = one_hot(jnp.logical_and(lines >= lanes * size, lines < lanes * size + size))
    sums = []
    for index in range(2):
        zero = jnp.zeros((tile_cols, channels), F32)
        carry = (zero, zero)
        for piece in range(2):
            loads[2 * index + piece].wait()

            def add(line, carry):
                values = tiles[index, line].astype(F32)
                return carry[0] + values, carry[1] + values * values

            carry = lax.fori_loop(piece * half, (piece + 1) * half, add, carry, unroll=4)
        sums += [jnp.sum(carry[0], axis=0, keepdims=True), jnp.sum(carry[1], axis=0, keepdims=True)]
    stacked = jnp.concatenate(sums + [jnp.zeros((4, channels), F32)], axis=0)
    grouped = jnp.dot(stacked, gather, precision=EXACT, preferred_element_type=F32)
    lane_part = lax.div(lax.broadcasted_iota(jnp.int32, (8, LANES), 1), GROUPS)
    kept = jnp.where(lane_part == lax.broadcasted_iota(jnp.int32, (8, LANES), 0), grouped, 0.0)
    part[...] = jnp.broadcast_to(jnp.sum(kept, axis=0, keepdims=True), (8, LANES))

    pl.semaphore_wait(barrier, first_peers + second_peers + 6)

    def send_sums(source, target, peer, count, phase):
        @pl.loop(1, count + 1)
        def _(step):
            pltpu.make_async_remote_copy(
                src_ref=source,
                dst_ref=target.at[step - 1],
                send_sem=sum_send.at[phase],
                recv_sem=sum_recv.at[phase],
                device_id=peer(step),
                device_id_type=pl.DeviceIdType.MESH,
            ).start()

    send_sums(part, part_in, first_peer, first_peers, 0)

    block = 16
    picks = lax.broadcasted_iota(jnp.int32, (2 * block, block * tile_cols), 0)
    cells = lax.broadcasted_iota(jnp.int32, (2 * block, block * tile_cols), 1)
    wanted = jnp.where(picks < block, picks * tile_cols, (picks - block) * tile_cols + tile_cols - 1)
    select = one_hot(cells == wanted, BF16)
    for index in range(2):
        for piece in range(tile_rows // block):
            span = pl.ds(piece * block, block)
            flat = tiles[index, span].reshape(block * tile_cols, channels)
            picked = jnp.dot(select, flat, preferred_element_type=F32).astype(BF16)
            cols[0, index, span] = picked[:block]
            cols[1, index, span] = picked[block:]

    head, tail = pl.ds(0, block), pl.ds(tile_rows - block, block)
    every = slice(None)
    moves = (
        (tiles.at[:, 0], rows_in.at[1], (up, col)),
        (tiles.at[:, tile_rows - 1], rows_in.at[0], (down, col)),
        (cols.at[0], cols_in.at[1], (row, left)),
        (cols.at[1], cols_in.at[0], (row, right)),
        (cols.at[0, every, head], corners_in.at[3], (up, left)),
        (cols.at[1, every, head], corners_in.at[2], (up, right)),
        (cols.at[0, every, tail], corners_in.at[1], (down, left)),
        (cols.at[1, every, tail], corners_in.at[0], (down, right)),
    )
    copies = []
    for index, (source, target, device) in enumerate(moves):
        copy = pltpu.make_async_remote_copy(
            src_ref=source,
            dst_ref=target,
            send_sem=side_send.at[index],
            recv_sem=side_recv.at[index],
            device_id=device,
            device_id_type=pl.DeviceIdType.MESH,
        )
        copy.start()
        copies.append(copy)

    total_wait(part_in, sum_recv.at[0])
    group[...] = part[...] + jnp.sum(part_in[...], axis=0)
    send_sums(group, group_in, second_peer, second_peers, 1)
    total_wait(group_in, sum_recv.at[1])
    totals = (group[...] + jnp.sum(group_in[...], axis=0)) / cell_count
    squares = pltpu.roll(totals, LANES - GROUPS, 1)
    means = lax.rem(lane_part, 2) == 0
    spread = lax.rsqrt(jnp.where(means, squares - totals * totals, 1.0) + EPSILON)
    lead = lax.broadcasted_iota(jnp.int32, (8, LANES), 0) == 0
    packed = jnp.where(lead, totals, spread)
    groups = lax.broadcasted_iota(jnp.int32, (LANES, channels), 0)
    members = lax.broadcasted_iota(jnp.int32, (LANES, channels), 1)
    factors = []
    for index, gain in enumerate((gain_one, gain_two)):
        own = (groups - 2 * GROUPS * index) * size
        valid = jnp.logical_and(groups >= 2 * GROUPS * index, groups < 2 * GROUPS * index + GROUPS)
        spill = one_hot(
            jnp.logical_and(valid, jnp.logical_and(members >= own, members < own + size))
        )
        spilt = jnp.dot(packed, spill, precision=EXACT, preferred_element_type=F32)
        factors.append((spilt[0:1], spilt[1:2] * gain[...] * 0.5))
    stats_out[...] = jnp.concatenate(
        [factors[0][0], factors[0][1], factors[1][0], factors[1][1], jnp.zeros((4, channels), F32)],
        axis=0,
    )

    for copy in copies:
        copy.wait_recv()

    outside_rows = (row == 0, row == n_row - 1)
    outside_cols = (col == 0, col == n_col - 1)
    for index, (center, scale) in enumerate(factors):

        def inner(strip, carry):
            above = tiles[index, strip * SH - 1].astype(F32)
            below = tiles[index, strip * SH].astype(F32)
            rows_out[index, 0, strip] = act(above, center, scale).astype(BF16)
            rows_out[index, 1, strip - 1] = act(below, center, scale).astype(BF16)
            return carry

        lax.fori_loop(1, strips, inner, 0)
        for side in range(2):
            value = act(rows_in[side, index].astype(F32), center, scale)
            value = jnp.where(outside_rows[side], 0.0, value)
            rows_out[index, side, side * (strips - 1)] = value.astype(BF16)
            value = act(cols_in[side, index].astype(F32), center, scale)
            value = jnp.where(outside_cols[side], 0.0, value)
            cols_out[index, side, 1 : tile_rows + 1] = value
            for end in range(2):
                value = act(corners_in[2 * end + side, index].astype(F32), center, scale)
                outside = jnp.logical_or(outside_cols[side], outside_rows[end])
                value = jnp.where(outside, 0.0, value)
                if end == 0:
                    cols_out[index, side, 0:1] = value[block - 1 : block]
                else:
                    cols_out[index, side, tile_rows + 1 : tile_rows + 2] = value[0:1]

    for copy in copies:
        copy.wait_send()
    total_wait(part_in, sum_send.at[0])
    total_wait(group_in, sum_send.at[1])


def margins(latent_shape, shape, stale_in, stale_hid, gain_one, gain_two):
    tile_rows, tile_cols, channels = latent_shape
    n_row, n_col = shape
    strips = tile_rows // SH
    cell_count = float(tile_rows * tile_cols * n_row * n_col * (channels // GROUPS))
    anywhere = pl.BlockSpec(memory_space=pl.ANY)
    vmem = pl.BlockSpec(memory_space=pltpu.VMEM)
    return pl.pallas_call(
        functools.partial(margins_kernel, cell_count, shape),
        out_shape=(
            jax.ShapeDtypeStruct((8, channels), F32),
            jax.ShapeDtypeStruct((2, 2, strips, tile_cols, channels), BF16),
            jax.ShapeDtypeStruct((2, 2, tile_rows + 16, channels), F32),
        ),
        in_specs=[anywhere, anywhere, vmem, vmem],
        out_specs=(vmem, vmem, vmem),
        scratch_shapes=[
            pltpu.VMEM((2, tile_rows, tile_cols, channels), BF16),
            pltpu.VMEM((2, 2, tile_rows, channels), BF16),
            pltpu.VMEM((2, 2, tile_cols, channels), BF16),
            pltpu.VMEM((2, 2, tile_rows, channels), BF16),
            pltpu.VMEM((4, 2, 16, channels), BF16),
            pltpu.VMEM((8, LANES), F32),
            pltpu.VMEM((2 * n_row - 1, 8, LANES), F32),
            pltpu.VMEM((8, LANES), F32),
            pltpu.VMEM((n_col // 2 - 1, 8, LANES), F32),
            pltpu.SemaphoreType.DMA((2, 2)),
            pltpu.SemaphoreType.DMA((8,)),
            pltpu.SemaphoreType.DMA((8,)),
            pltpu.SemaphoreType.DMA((2,)),
            pltpu.SemaphoreType.DMA((2,)),
        ],
        compiler_params=pltpu.CompilerParams(
            collective_id=0, has_side_effects=True, vmem_limit_bytes=24 * 2**20
        ),
        name="margins",
    )(stale_in, stale_hid, gain_one, gain_two)


def strips_kernel(
    refresh,
    stats,
    rows,
    cols,
    shift,
    latent,
    stale_hid,
    weight_one,
    weight_two,
    block_out,
    hidden_out,
    tile,
    weights,
    frame,
    window,
    hidden,
    finished,
    load_sem,
    store_sem,
):
    tile_rows, tile_cols, channels = tile.shape
    strips = tile_rows // SH
    loads = [pltpu.make_async_copy(latent, tile, load_sem.at[0])]
    for index, source in enumerate((weight_one, weight_two)):
        loads.append(
            pltpu.make_async_copy(
                source, weights.at[index, :, pl.ds(0, channels)], load_sem.at[1 + index]
            )
        )
    for copy in loads:
        copy.start()
    wide = weights.shape[2]
    weights[:, :, channels:] = jnp.zeros(weights.shape[:2] + (wide - channels, channels), BF16)
    window[:, :, :, channels:] = jnp.zeros(window.shape[:3] + (wide - channels,), BF16)
    for copy in loads:
        copy.wait()

    def convolve(index, strip, inner):
        frame[0, 8 : tile_cols + 8] = rows[index, 0, strip].astype(F32)
        frame[SH + 1, 8 : tile_cols + 8] = rows[index, 1, strip].astype(F32)
        frame[1 : SH + 1, 8 : tile_cols + 8] = inner
        for line in range(SH + 2):
            place = pl.ds(strip * SH + line, 1)
            frame[line, 7:8] = cols[index, 0, place]
            frame[line, tile_cols + 8 : tile_cols + 9] = cols[index, 1, place]
        for offset in range(3):
            window[offset, :, :, :channels] = frame[:, 7 + offset : 7 + offset + tile_cols].astype(
                BF16
            )
        taps = [
            window[tap % 3, tap // 3 : tap // 3 + SH].reshape(SH * tile_cols, wide)
            for tap in range(9)
        ]
        return jnp.dot(
            jnp.concatenate(taps, axis=1),
            weights[index].reshape(9 * wide, channels),
            preferred_element_type=F32,
        )

    def one_strip(strip, carry):
        span = pl.ds(strip * SH, SH)
        base = tile[span].astype(F32)
        first = convolve(0, strip, act(base, stats[0:1], stats[1:2]))
        fresh = (first + shift[...]).astype(BF16).reshape(SH, tile_cols, channels)
        hidden[span] = fresh
        second = convolve(1, strip, act(fresh.astype(F32), stats[2:3], stats[3:4]))
        done = tile[span].astype(F32) + second.reshape(SH, tile_cols, channels)
        finished[span] = done.astype(BF16)
        live = refresh[strip, 0] > 0

        @pl.when(live)
        def _():
            pltpu.make_async_copy(hidden.at[span], hidden_out.at[span], store_sem.at[0]).start()
            pltpu.make_async_copy(finished.at[span], block_out.at[span], store_sem.at[1]).start()

        @pl.when(jnp.logical_not(live))
        def _():
            pltpu.make_async_copy(stale_hid.at[span], hidden_out.at[span], store_sem.at[0]).start()
            pltpu.make_async_copy(tile.at[span], block_out.at[span], store_sem.at[1]).start()

        return carry

    lax.fori_loop(0, strips, one_strip, 0)
    total_wait(hidden, store_sem.at[0])
    total_wait(finished, store_sem.at[1])


def refreshed(refresh, stats, rows, cols, shift, latent, stale_hid, weight_one, weight_two):
    tile_rows, tile_cols, channels = latent.shape
    wide = -(-channels // LANES) * LANES
    anywhere = pl.BlockSpec(memory_space=pl.ANY)
    vmem = pl.BlockSpec(memory_space=pltpu.VMEM)
    tile = jax.ShapeDtypeStruct(latent.shape, BF16)
    return pl.pallas_call(
        strips_kernel,
        out_shape=(tile, tile),
        in_specs=[pl.BlockSpec(memory_space=pltpu.SMEM)] + [vmem] * 4 + [anywhere] * 4,
        out_specs=(anywhere, anywhere),
        scratch_shapes=[
            pltpu.VMEM(latent.shape, BF16),
            pltpu.VMEM((2, 9, wide, channels), BF16),
            pltpu.VMEM((SH + 2, tile_cols + 16, channels), F32),
            pltpu.VMEM((3, SH + 2, tile_cols, wide), BF16),
            pltpu.VMEM(latent.shape, BF16),
            pltpu.VMEM(latent.shape, BF16),
            pltpu.SemaphoreType.DMA((3,)),
            pltpu.SemaphoreType.DMA((2,)),
        ],
        compiler_params=pltpu.CompilerParams(vmem_limit_bytes=48 * 2**20),
        name="strips",
    )(refresh, stats, rows, cols, shift, latent, stale_hid, weight_one, weight_two)


def per_device(
    shape,
    latent,
    stale_input,
    stale_hidden,
    refresh,
    gain_one,
    weight_one,
    time_shift,
    gain_two,
    weight_two,
):
    stats, rows, cols = margins(
        latent.shape, shape, stale_input, stale_hidden, gain_one[None], gain_two[None]
    )
    return refreshed(
        refresh, stats, rows, cols, time_shift[None], latent, stale_hidden, weight_one, weight_two
    )


def solution(mesh):
    placed = (
        P("row", "col", None),
        P("row", "col", None),
        P("row", "col", None),
        P("row", "col"),
        P(),
        P(),
        P(),
        P(),
        P(),
    )
    return jax.shard_map(
        functools.partial(per_device, (mesh.shape["row"], mesh.shape["col"])),
        mesh=mesh,
        in_specs=placed,
        out_specs=(P("row", "col", None), P("row", "col", None)),
        check_vma=False,
    )
```

```python
import functools

import jax
import jax.numpy as jnp
from jax import lax
from jax.experimental import pallas as pl
from jax.experimental.pallas import tpu as pltpu
from jax.sharding import PartitionSpec as P

GROUPS = 32
SH = 8
EPSILON = 1e-05
LANES = 128
EXACT = lax.Precision.HIGHEST
F32 = jnp.float32
BF16 = jnp.bfloat16
MAIN = 256
AHEAD = 4
DEPTH = 1


def act(values, center, half_scale):
    half = (values - center) * half_scale
    return half * jnp.tanh(half) + half


def one_hot(condition, kind=F32):
    return jnp.where(condition, 1.0, 0.0).astype(kind)


def total_wait(buffer, semaphore):
    pltpu.make_async_copy(buffer, buffer, semaphore).wait()


def tails(values):
    rest = values[..., MAIN:]
    blank = jnp.zeros(rest.shape[:-1] + (LANES - rest.shape[-1],), rest.dtype)
    return jnp.concatenate([rest, blank], axis=-1)


def side_by_side(main, rest):
    turned = pltpu.roll(rest[1], LANES // 2, rest[1].ndim - 1)
    pairs = (rest[0] + turned).astype(BF16)
    return jnp.concatenate([*main, pairs, rest[2].astype(BF16)], axis=-1)


def margins_kernel(
    cell_count,
    shape,
    stale_in,
    stale_hid,
    latent,
    weight_one,
    weight_two,
    gain_one,
    gain_two,
    stats_out,
    rows_out,
    cols_out,
    tile_out,
    first_weights,
    second_weights,
    first_gain,
    second_gain,
    tiles,
    laid_out,
    raw,
    cols,
    rows_in,
    cols_in,
    corners_in,
    part,
    part_in,
    group,
    group_in,
    load_sem,
    late_sem,
    leave_sem,
    side_send,
    side_recv,
    sum_send,
    sum_recv,
):
    n_row, n_col = shape
    row, col = lax.axis_index("row"), lax.axis_index("col")
    tile_rows, tile_cols, channels = tiles.shape[1:]
    strips = tile_rows // SH
    up, down = lax.rem(row + n_row - 1, n_row), lax.rem(row + 1, n_row)
    left, right = lax.rem(col + n_col - 1, n_col), lax.rem(col + 1, n_col)
    core, x_high, z = lax.rem(col, 2), lax.rem(lax.div(col, 2), 2), lax.div(col, 4)
    y, x = lax.rem(row, 4), x_high * 2 + lax.div(row, 4)
    deep = n_col // 4
    first_peers, second_peers = 2 * deep - 1, 2 * n_row - 1

    def first_peer(step):
        place = lax.rem(z * 2 + core + lax.rem(step + deep - 1, first_peers) + 1, 2 * deep)
        return row, lax.div(place, 2) * 4 + x_high * 2 + lax.rem(place, 2)

    def second_peer(step):
        offset = lax.rem(step + 9, second_peers) + 1
        there_x, there_y = lax.rem(x + lax.div(offset, 4), 4), lax.rem(y + lax.rem(offset, 4), 4)
        there_row = lax.rem(there_x, 2) * 4 + there_y
        return there_row, z * 4 + lax.div(there_x, 2) * 2 + core

    def signal(device):
        pl.semaphore_signal(
            barrier, inc=1, device_id=device, device_id_type=pl.DeviceIdType.MESH
        )

    loads = []
    half = tile_rows // 2
    for index, source in enumerate((stale_in, stale_hid)):
        for piece in range(2):
            span = pl.ds(piece * half, half)
            copy = pltpu.make_async_copy(
                source.at[span], tiles.at[index, span], load_sem.at[index, piece]
            )
            copy.start()
            loads.append(copy)

    late = [
        pltpu.make_async_copy(weight_one, raw.at[0], late_sem.at[0]),
        pltpu.make_async_copy(weight_two, raw.at[1], late_sem.at[1]),
        pltpu.make_async_copy(latent, tile_out, late_sem.at[2]),
        pltpu.make_async_copy(gain_one, first_gain, late_sem.at[3]),
        pltpu.make_async_copy(gain_two, second_gain, late_sem.at[4]),
    ]
    for copy in late:
        copy.start()

    barrier = pltpu.get_barrier_semaphore()

    @pl.loop(0, first_peers)
    def _(step):
        signal(first_peer(step))
        signal(second_peer(step))

    for place in (up, row, down):
        for device in ((place, left), (place, right)):
            signal(device)
    signal((up, col))
    signal((down, col))

    lines = lax.broadcasted_iota(jnp.int32, (channels, LANES), 0)
    lanes = lax.rem(lax.broadcasted_iota(jnp.int32, (channels, LANES), 1), GROUPS)
    size = channels // GROUPS
    gather = one_hot(jnp.logical_and(lines >= lanes * size, lines < lanes * size + size))
    sums = []
    for index in range(2):
        zero = jnp.zeros((tile_cols, channels), F32)
        carry = (zero, zero)
        for piece in range(2):
            loads[2 * index + piece].wait()

            def add(line, carry):
                values = tiles[index, line].astype(F32)
                return carry[0] + values, carry[1] + values * values

            carry = lax.fori_loop(piece * half, (piece + 1) * half, add, carry, unroll=4)
        sums += [jnp.sum(carry[0], axis=0, keepdims=True), jnp.sum(carry[1], axis=0, keepdims=True)]
    stacked = jnp.concatenate(sums + [jnp.zeros((4, channels), F32)], axis=0)
    grouped = jnp.dot(stacked, gather, precision=EXACT, preferred_element_type=F32)
    lane_part = lax.div(lax.broadcasted_iota(jnp.int32, (8, LANES), 1), GROUPS)
    kept = jnp.where(lane_part == lax.broadcasted_iota(jnp.int32, (8, LANES), 0), grouped, 0.0)
    part[...] = jnp.broadcast_to(jnp.sum(kept, axis=0, keepdims=True), (8, LANES))

    pl.semaphore_wait(barrier, first_peers + second_peers + 8)

    def send_sums(source, target, peer, count, phase):
        @pl.loop(0, count)
        def _(step):
            pltpu.make_async_remote_copy(
                src_ref=source.at[0:1],
                dst_ref=target.at[step, 0:1],
                send_sem=sum_send.at[phase],
                recv_sem=sum_recv.at[phase],
                device_id=peer(step),
                device_id_type=pl.DeviceIdType.MESH,
            ).start()

    send_sums(part, part_in, first_peer, first_peers, 0)

    block = 16
    picks = lax.broadcasted_iota(jnp.int32, (2 * block, block * tile_cols), 0)
    cells = lax.broadcasted_iota(jnp.int32, (2 * block, block * tile_cols), 1)
    wanted = jnp.where(picks < block, picks * tile_cols, (picks - block) * tile_cols + tile_cols - 1)
    select = one_hot(cells == wanted, BF16)
    for index in range(2):
        for piece in range(tile_rows // block):
            span = pl.ds(piece * block, block)
            flat = tiles[index, span].reshape(block * tile_cols, channels)
            picked = jnp.dot(select, flat, preferred_element_type=F32).astype(BF16)
            cols[0, index, span] = picked[:block]
            cols[1, index, span] = picked[block:]

    head, tail = pl.ds(0, block), pl.ds(tile_rows - block, block)
    every = slice(None)
    moves = (
        (tiles.at[:, 0], rows_in.at[1], (up, col)),
        (tiles.at[:, tile_rows - 1], rows_in.at[0], (down, col)),
        (cols.at[0], cols_in.at[1], (row, left)),
        (cols.at[1], cols_in.at[0], (row, right)),
        (cols.at[0, every, head], corners_in.at[3], (up, left)),
        (cols.at[1, every, head], corners_in.at[2], (up, right)),
        (cols.at[0, every, tail], corners_in.at[1], (down, left)),
        (cols.at[1, every, tail], corners_in.at[0], (down, right)),
    )
    copies = []
    for index, (source, target, device) in enumerate(moves):
        copy = pltpu.make_async_remote_copy(
            src_ref=source,
            dst_ref=target,
            send_sem=side_send.at[index],
            recv_sem=side_recv.at[index],
            device_id=device,
            device_id_type=pl.DeviceIdType.MESH,
        )
        copy.start()
        copies.append(copy)

    leaving = []
    for index in range(2):
        late[index].wait()
        target = laid_out.at[index]
        for down_tap in range(3):
            taps = [raw[index, 3 * down_tap + across] for across in range(3)]
            rest = [tap[:, MAIN:] for tap in taps]
            blank = jnp.zeros_like(rest[0])
            ends = jnp.concatenate(rest + [blank], axis=1)
            pieces = [tap[:, :MAIN] for tap in taps] + [ends]
            for place, piece in enumerate(pieces):
                lanes = pl.ds(place * MAIN, MAIN)
                target[pl.ds(down_tap * MAIN, MAIN), lanes] = piece[:MAIN]
                spot = pl.ds(3 * MAIN + down_tap * (channels - MAIN), channels - MAIN)
                target[spot, lanes] = piece[MAIN:]
        spot = pl.ds(3 * channels, 4 * MAIN - 3 * channels)
        target[spot] = jnp.zeros((4 * MAIN - 3 * channels, 4 * MAIN), BF16)
        out = (first_weights, second_weights)[index]
        copy = pltpu.make_async_copy(target, out, leave_sem.at[index])
        copy.start()
        leaving.append(copy)
    late[2].wait()
    late[3].wait()
    late[4].wait()

    total_wait(part_in.at[:, 0:1], sum_recv.at[0])
    group[0:1] = part[0:1] + jnp.sum(part_in[:, 0:1], axis=0)
    send_sums(group, group_in, second_peer, second_peers, 1)
    total_wait(group_in.at[:, 0:1], sum_recv.at[1])
    totals = jnp.broadcast_to(group[0:1] + jnp.sum(group_in[:, 0:1], axis=0), (8, LANES)) / cell_count
    squares = pltpu.roll(totals, LANES - GROUPS, 1)
    means = lax.rem(lane_part, 2) == 0
    spread = lax.rsqrt(jnp.where(means, squares - totals * totals, 1.0) + EPSILON)
    lead = lax.broadcasted_iota(jnp.int32, (8, LANES), 0) == 0
    packed = jnp.where(lead, totals, spread)
    groups = lax.broadcasted_iota(jnp.int32, (LANES, channels), 0)
    members = lax.broadcasted_iota(jnp.int32, (LANES, channels), 1)
    factors = []
    for index, gain in enumerate((first_gain, second_gain)):
        own = (groups - 2 * GROUPS * index) * size
        valid = jnp.logical_and(groups >= 2 * GROUPS * index, groups < 2 * GROUPS * index + GROUPS)
        spill = one_hot(
            jnp.logical_and(valid, jnp.logical_and(members >= own, members < own + size))
        )
        spilt = jnp.dot(packed, spill, precision=EXACT, preferred_element_type=F32)
        factors.append((spilt[0:1], spilt[1:2] * gain[...].reshape(1, channels) * 0.5))
    stats_out[...] = jnp.concatenate(
        [factors[0][0], factors[0][1], factors[1][0], factors[1][1], jnp.zeros((4, channels), F32)],
        axis=0,
    )

    for copy in copies:
        copy.wait_recv()

    outside_rows = (row == 0, row == n_row - 1)
    outside_cols = (col == 0, col == n_col - 1)
    for index, (center, scale) in enumerate(factors):

        def inner(strip, carry):
            above = tiles[index, strip * SH - 1].astype(F32)
            below = tiles[index, strip * SH].astype(F32)
            rows_out[index, 0, strip] = act(above, center, scale).astype(BF16)
            rows_out[index, 1, strip - 1] = act(below, center, scale).astype(BF16)
            return carry

        lax.fori_loop(1, strips, inner, 0)
        for side in range(2):
            value = act(rows_in[side, index].astype(F32), center, scale)
            value = jnp.where(outside_rows[side], 0.0, value)
            rows_out[index, side, side * (strips - 1)] = value.astype(BF16)
            value = act(cols_in[side, index].astype(F32), center, scale)
            value = jnp.where(outside_cols[side], 0.0, value)
            cols_out[index, side, 1 : tile_rows + 1] = value
            for end in range(2):
                value = act(corners_in[2 * end + side, index].astype(F32), center, scale)
                outside = jnp.logical_or(outside_cols[side], outside_rows[end])
                value = jnp.where(outside, 0.0, value)
                if end == 0:
                    cols_out[index, side, 0:1] = value[block - 1 : block]
                else:
                    cols_out[index, side, tile_rows + 1 : tile_rows + 2] = value[0:1]

    for copy in leaving:
        copy.wait()
    for copy in copies:
        copy.wait_send()
    total_wait(part_in.at[:, 0:1], sum_send.at[0])
    total_wait(group_in.at[:, 0:1], sum_send.at[1])


def margins(shape, stale_in, stale_hid, latent, weight_one, weight_two, gain_one, gain_two):
    tile_rows, tile_cols, channels = latent.shape
    n_row, n_col = shape
    strips = tile_rows // SH
    cell_count = float(tile_rows * tile_cols * n_row * n_col * (channels // GROUPS))
    hbm = pl.BlockSpec(memory_space=pltpu.HBM)
    vmem = pl.BlockSpec(memory_space=pltpu.VMEM)
    return pl.pallas_call(
        functools.partial(margins_kernel, cell_count, shape),
        out_shape=(
            jax.ShapeDtypeStruct((8, channels), F32),
            jax.ShapeDtypeStruct((2, 2, strips, tile_cols, channels), BF16),
            jax.ShapeDtypeStruct((2, 2, tile_rows + 16, channels), F32),
            jax.ShapeDtypeStruct((tile_rows, tile_cols, channels), BF16),
            jax.ShapeDtypeStruct((4 * MAIN, 4 * MAIN), BF16),
            jax.ShapeDtypeStruct((4 * MAIN, 4 * MAIN), BF16),
        ),
        in_specs=[hbm] * 7,
        out_specs=(vmem,) * 4 + (hbm,) * 2,
        scratch_shapes=[
            pltpu.VMEM((channels,), F32),
            pltpu.VMEM((channels,), F32),
            pltpu.VMEM((2, tile_rows, tile_cols, channels), BF16),
            pltpu.VMEM((2, 4 * MAIN, 4 * MAIN), BF16),
            pltpu.VMEM((2,) + weight_one.shape, BF16),
            pltpu.VMEM((2, 2, tile_rows, channels), BF16),
            pltpu.VMEM((2, 2, tile_cols, channels), BF16),
            pltpu.VMEM((2, 2, tile_rows, channels), BF16),
            pltpu.VMEM((4, 2, 16, channels), BF16),
            pltpu.VMEM((8, LANES), F32),
            pltpu.VMEM((n_col // 2 - 1, 8, LANES), F32),
            pltpu.VMEM((8, LANES), F32),
            pltpu.VMEM((2 * n_row - 1, 8, LANES), F32),
            pltpu.SemaphoreType.DMA((2, 2)),
            pltpu.SemaphoreType.DMA((5,)),
            pltpu.SemaphoreType.DMA((2,)),
            pltpu.SemaphoreType.DMA((8,)),
            pltpu.SemaphoreType.DMA((8,)),
            pltpu.SemaphoreType.DMA((2,)),
            pltpu.SemaphoreType.DMA((2,)),
        ],
        compiler_params=pltpu.CompilerParams(
            collective_id=0, has_side_effects=True, vmem_limit_bytes=50 * 2**20
        ),
        name="margins",
    )(stale_in, stale_hid, latent, weight_one, weight_two, gain_one, gain_two)


def strips_kernel(
    refresh,
    stats,
    rows,
    cols,
    shift,
    tile,
    far_first,
    far_second,
    far_hidden,
    block_out,
    hidden_out,
    first_weights,
    second_weights,
    stale_hid,
    sides,
    hidden,
    finished,
    load_sem,
    store_sem,
):
    tile_rows, tile_cols, channels = tile.shape
    strips = tile_rows // SH
    cells = SH * tile_cols
    packs = cells // 8
    apart = tile_cols // 8
    loads = [
        pltpu.make_async_copy(far_first, first_weights, load_sem.at[0]),
        pltpu.make_async_copy(far_second, second_weights, load_sem.at[1]),
        pltpu.make_async_copy(far_hidden, stale_hid, load_sem.at[2]),
    ]
    for copy in loads:
        copy.start()
    weights = (first_weights, second_weights)

    def margin_terms(index):
        for side in range(2):
            parts = [cols[index, side, a : a + tile_rows] for a in range(3)]
            lhs = side_by_side([part[:, :MAIN].astype(BF16) for part in parts], [tails(part) for part in parts])
            start = 2 * MAIN * side
            sides[index, side, :, :MAIN] = jnp.dot(
                lhs, weights[index][:, start : start + MAIN], preferred_element_type=F32
            )
            start = 3 * MAIN + LANES * side
            sides[index, side, :, MAIN:] = jnp.dot(
                lhs, weights[index][:, start : start + LANES], preferred_element_type=F32
            )
    sub = lax.broadcasted_iota(jnp.int32, (1, 8, 1), 1)

    def moved(index, side, strip, part, lanes):
        width = part.shape[-1]
        turned = pltpu.roll(part.reshape(packs, 8, width), 1 if side == 0 else 7, 1)
        pieces = []
        for line in range(SH):
            edge = jnp.broadcast_to(
                sides[index, side, strip * SH + line : strip * SH + line + 1, lanes], (8, width)
            )[None]
            first = line * apart
            if side == 0:
                pieces += [edge, turned[first : first + apart - 1]]
            else:
                pieces += [turned[first + 1 : first + apart], edge]
        carried = jnp.concatenate(pieces, axis=0)
        at = 0 if side == 0 else 7
        return jnp.where(sub == at, carried, turned).reshape(cells, width)

    def multiply(index, strip, inner):
        above, below = rows[index, 0, strip].astype(F32), rows[index, 1, strip].astype(F32)
        values = jnp.concatenate([above[None], inner, below[None]], axis=0)
        main = values[..., :MAIN].astype(BF16)
        rest = tails(values)
        wide = side_by_side(
            [main[a : a + SH] for a in range(3)], [rest[a : a + SH] for a in range(3)]
        ).reshape(cells, 4 * MAIN)
        return [
            jnp.dot(
                wide,
                weights[index][:, part * MAIN : (part + 1) * MAIN],
                preferred_element_type=F32,
            )
            for part in range(4)
        ]

    def collect(index, strip, products):
        early, same, late, rest = products
        low, high = slice(0, MAIN), slice(MAIN, MAIN + LANES)
        main = moved(index, 0, strip, early, low) + same + moved(index, 1, strip, late, low)
        ends = (
            moved(index, 0, strip, rest[:, :LANES], high)
            + pltpu.roll(rest[:, :LANES], LANES // 2, 1)
            + moved(index, 1, strip, rest[:, LANES:], high)
        )
        return jnp.concatenate([main, ends[:, : channels - MAIN]], axis=1)

    fresh = {}

    def begin(index, strip):
        span = slice(strip * SH, strip * SH + SH)
        if index == 0:
            inner = act(tile[span].astype(F32), stats[0:1], stats[1:2])
        else:
            inner = act(fresh[strip].astype(F32), stats[2:3], stats[3:4])
        return multiply(index, strip, inner)

    def finish(index, strip, products):
        span = slice(strip * SH, strip * SH + SH)
        live = refresh[0, strip] > 0
        summed = collect(index, strip, products)
        if index == 0:
            value = (summed + shift[...].reshape(1, channels)).astype(BF16).reshape(SH, tile_cols, channels)
            fresh[strip] = value
            hidden[span] = jnp.where(live, value, stale_hid[span])
            made, out = hidden, hidden_out
        else:
            value = tile[span].astype(F32) + summed.reshape(SH, tile_cols, channels)
            finished[span] = jnp.where(live, value.astype(BF16), tile[span])
            made, out = finished, block_out
        pltpu.make_async_copy(made.at[span], out.at[span], store_sem.at[index]).start()

    loads[0].wait()
    margin_terms(0)
    jobs = [(index, strip) for half in range(0, strips, AHEAD) for index in range(2) for strip in range(half, half + AHEAD)]
    waiting, done = [], []
    for job in jobs:
        waiting.append((*job, begin(*job)))
        if len(waiting) > DEPTH:
            if len(done) == 0:
                for copy in loads[1:]:
                    copy.wait()
                margin_terms(1)
            done.append(waiting[0][:2])
            finish(*waiting.pop(0))
    for job in waiting:
        finish(*job)
    total_wait(hidden, store_sem.at[0])
    total_wait(finished, store_sem.at[1])


def refreshed(
    refresh, stats, rows, cols, shift, tile, first_weights, second_weights, stale_hid
):
    tile_shape = tile.shape
    tile_rows, tile_cols, channels = tile_shape
    anywhere = pl.BlockSpec(memory_space=pl.ANY)
    vmem = pl.BlockSpec(memory_space=pltpu.VMEM)
    out = jax.ShapeDtypeStruct(tile_shape, BF16)
    return pl.pallas_call(
        strips_kernel,
        out_shape=(out, out),
        in_specs=[pl.BlockSpec(memory_space=pltpu.SMEM)] + [vmem] * 5 + [anywhere] * 3,
        out_specs=(anywhere, anywhere),
        scratch_shapes=[
            pltpu.VMEM((4 * MAIN, 4 * MAIN), BF16),
            pltpu.VMEM((4 * MAIN, 4 * MAIN), BF16),
            pltpu.VMEM(tile_shape, BF16),
            pltpu.VMEM((2, 2, tile_rows, MAIN + LANES), F32),
            pltpu.VMEM(tile_shape, BF16),
            pltpu.VMEM(tile_shape, BF16),
            pltpu.SemaphoreType.DMA((3,)),
            pltpu.SemaphoreType.DMA((2,)),
        ],
        compiler_params=pltpu.CompilerParams(vmem_limit_bytes=50 * 2**20),
        name="strips",
    )(refresh, stats, rows, cols, shift, tile, first_weights, second_weights, stale_hid)


def per_device(
    shape,
    latent,
    stale_input,
    stale_hidden,
    refresh,
    gain_one,
    weight_one,
    time_shift,
    gain_two,
    weight_two,
):
    stats, rows, cols, tile, first_weights, second_weights = margins(
        shape, stale_input, stale_hidden, latent, weight_one, weight_two, gain_one, gain_two
    )
    return refreshed(
        refresh.T, stats, rows, cols, time_shift, tile, first_weights, second_weights, stale_hidden
    )


def solution(mesh):
    placed = (
        P("row", "col", None),
        P("row", "col", None),
        P("row", "col", None),
        P("row", "col"),
        P(),
        P(),
        P(),
        P(),
        P(),
    )
    return jax.shard_map(
        functools.partial(per_device, (mesh.shape["row"], mesh.shape["col"])),
        mesh=mesh,
        in_specs=placed,
        out_specs=(P("row", "col", None), P("row", "col", None)),
        check_vma=False,
    )
```

```python
import functools

import jax
import jax.numpy as jnp
from jax import lax
from jax.experimental import pallas as pl
from jax.experimental.pallas import tpu as pltpu
from jax.sharding import PartitionSpec as P

GROUPS = 32
SH = 8
EPSILON = 1e-05
LANES = 128
EXACT = lax.Precision.HIGHEST
F32 = jnp.float32
BF16 = jnp.bfloat16
MAIN = 256
AHEAD = 4
DEPTH = 1


def act(values, center, half_scale):
    half = (values - center) * half_scale
    return half * jnp.tanh(half) + half


def one_hot(condition, kind=F32):
    return jnp.where(condition, 1.0, 0.0).astype(kind)


def total_wait(buffer, semaphore):
    pltpu.make_async_copy(buffer, buffer, semaphore).wait()


def tails(values):
    rest = values[..., MAIN:]
    blank = jnp.zeros(rest.shape[:-1] + (LANES - rest.shape[-1],), rest.dtype)
    return jnp.concatenate([rest, blank], axis=-1)


def side_by_side(main, rest):
    turned = pltpu.roll(rest[1], LANES // 2, rest[1].ndim - 1)
    pairs = (rest[0] + turned).astype(BF16)
    return jnp.concatenate([*main, pairs, rest[2].astype(BF16)], axis=-1)


def margins_kernel(
    cell_count,
    shape,
    stale_in,
    stale_hid,
    latent,
    weight_one,
    weight_two,
    totals_out,
    rows_out,
    cols_out,
    tile_out,
    first_weights,
    second_weights,
    tiles,
    laid_out,
    raw,
    cols,
    rows_in,
    cols_in,
    corners_in,
    part,
    part_in,
    group,
    group_in,
    load_sem,
    late_sem,
    leave_sem,
    side_send,
    side_recv,
    sum_send,
    sum_recv,
):
    n_row, n_col = shape
    row, col = lax.axis_index("row"), lax.axis_index("col")
    tile_rows, tile_cols, channels = tiles.shape[1:]
    strips = tile_rows // SH
    up, down = lax.rem(row + n_row - 1, n_row), lax.rem(row + 1, n_row)
    left, right = lax.rem(col + n_col - 1, n_col), lax.rem(col + 1, n_col)
    core, x_high, z = lax.rem(col, 2), lax.rem(lax.div(col, 2), 2), lax.div(col, 4)
    y, x = lax.rem(row, 4), x_high * 2 + lax.div(row, 4)
    deep = n_col // 4
    first_peers, second_peers = 2 * deep - 1, 2 * n_row - 1

    def first_peer(step):
        place = lax.rem(z * 2 + core + lax.rem(step + deep - 1, first_peers) + 1, 2 * deep)
        return row, lax.div(place, 2) * 4 + x_high * 2 + lax.rem(place, 2)

    def second_peer(step):
        offset = lax.rem(step + 9, second_peers) + 1
        there_x, there_y = lax.rem(x + lax.div(offset, 4), 4), lax.rem(y + lax.rem(offset, 4), 4)
        there_row = lax.rem(there_x, 2) * 4 + there_y
        return there_row, z * 4 + lax.div(there_x, 2) * 2 + core

    def signal(device):
        pl.semaphore_signal(
            barrier, inc=1, device_id=device, device_id_type=pl.DeviceIdType.MESH
        )

    loads = []
    half = tile_rows // 2
    for index, source in enumerate((stale_in, stale_hid)):
        for piece in range(2):
            span = pl.ds(piece * half, half)
            copy = pltpu.make_async_copy(
                source.at[span], tiles.at[index, span], load_sem.at[index, piece]
            )
            copy.start()
            loads.append(copy)

    late = [
        pltpu.make_async_copy(weight_one, raw.at[0], late_sem.at[0]),
        pltpu.make_async_copy(weight_two, raw.at[1], late_sem.at[1]),
        pltpu.make_async_copy(latent, tile_out, late_sem.at[2]),
    ]
    for copy in late:
        copy.start()

    barrier = pltpu.get_barrier_semaphore()

    @pl.loop(0, first_peers)
    def _(step):
        signal(first_peer(step))
        signal(second_peer(step))

    for place in (up, row, down):
        for device in ((place, left), (place, right)):
            signal(device)
    signal((up, col))
    signal((down, col))

    lines = lax.broadcasted_iota(jnp.int32, (channels, LANES), 0)
    lanes = lax.rem(lax.broadcasted_iota(jnp.int32, (channels, LANES), 1), GROUPS)
    size = channels // GROUPS
    gather = one_hot(jnp.logical_and(lines >= lanes * size, lines < lanes * size + size))
    sums = []
    for index in range(2):
        zero = jnp.zeros((tile_cols, channels), F32)
        carry = (zero, zero)
        for piece in range(2):
            loads[2 * index + piece].wait()

            def add(line, carry):
                values = tiles[index, line].astype(F32)
                return carry[0] + values, carry[1] + values * values

            carry = lax.fori_loop(piece * half, (piece + 1) * half, add, carry, unroll=4)
        sums += [jnp.sum(carry[0], axis=0, keepdims=True), jnp.sum(carry[1], axis=0, keepdims=True)]
    stacked = jnp.concatenate(sums + [jnp.zeros((4, channels), F32)], axis=0)
    grouped = jnp.dot(stacked, gather, precision=EXACT, preferred_element_type=F32)
    lane_part = lax.div(lax.broadcasted_iota(jnp.int32, (8, LANES), 1), GROUPS)
    kept = jnp.where(lane_part == lax.broadcasted_iota(jnp.int32, (8, LANES), 0), grouped, 0.0)
    part[...] = jnp.broadcast_to(jnp.sum(kept, axis=0, keepdims=True), (8, LANES))

    pl.semaphore_wait(barrier, first_peers + second_peers + 8)

    def send_sums(source, target, peer, count, phase):
        @pl.loop(0, count)
        def _(step):
            pltpu.make_async_remote_copy(
                src_ref=source.at[0:1],
                dst_ref=target.at[step, 0:1],
                send_sem=sum_send.at[phase],
                recv_sem=sum_recv.at[phase],
                device_id=peer(step),
                device_id_type=pl.DeviceIdType.MESH,
            ).start()

    send_sums(part, part_in, first_peer, first_peers, 0)

    block = 16
    picks = lax.broadcasted_iota(jnp.int32, (2 * block, block * tile_cols), 0)
    cells = lax.broadcasted_iota(jnp.int32, (2 * block, block * tile_cols), 1)
    wanted = jnp.where(picks < block, picks * tile_cols, (picks - block) * tile_cols + tile_cols - 1)
    select = one_hot(cells == wanted, BF16)
    for index in range(2):
        for piece in range(tile_rows // block):
            span = pl.ds(piece * block, block)
            flat = tiles[index, span].reshape(block * tile_cols, channels)
            picked = jnp.dot(select, flat, preferred_element_type=F32).astype(BF16)
            cols[0, index, span] = picked[:block]
            cols[1, index, span] = picked[block:]

    head, tail = pl.ds(0, block), pl.ds(tile_rows - block, block)
    every = slice(None)
    moves = (
        (tiles.at[:, 0], rows_in.at[1], (up, col)),
        (tiles.at[:, tile_rows - 1], rows_in.at[0], (down, col)),
        (cols.at[0], cols_in.at[1], (row, left)),
        (cols.at[1], cols_in.at[0], (row, right)),
        (cols.at[0, every, head], corners_in.at[3], (up, left)),
        (cols.at[1, every, head], corners_in.at[2], (up, right)),
        (cols.at[0, every, tail], corners_in.at[1], (down, left)),
        (cols.at[1, every, tail], corners_in.at[0], (down, right)),
    )
    copies = []
    for index, (source, target, device) in enumerate(moves):
        copy = pltpu.make_async_remote_copy(
            src_ref=source,
            dst_ref=target,
            send_sem=side_send.at[index],
            recv_sem=side_recv.at[index],
            device_id=device,
            device_id_type=pl.DeviceIdType.MESH,
        )
        copy.start()
        copies.append(copy)

    leaving = []
    for index in range(2):
        late[index].wait()
        target = laid_out.at[index]
        for down_tap in range(3):
            taps = [raw[index, 3 * down_tap + across] for across in range(3)]
            rest = [tap[:, MAIN:] for tap in taps]
            blank = jnp.zeros_like(rest[0])
            ends = jnp.concatenate(rest + [blank], axis=1)
            pieces = [tap[:, :MAIN] for tap in taps] + [ends]
            for place, piece in enumerate(pieces):
                lanes = pl.ds(place * MAIN, MAIN)
                target[pl.ds(down_tap * MAIN, MAIN), lanes] = piece[:MAIN]
                spot = pl.ds(3 * MAIN + down_tap * (channels - MAIN), channels - MAIN)
                target[spot, lanes] = piece[MAIN:]
        spot = pl.ds(3 * channels, 4 * MAIN - 3 * channels)
        target[spot] = jnp.zeros((4 * MAIN - 3 * channels, 4 * MAIN), BF16)
        out = (first_weights, second_weights)[index]
        copy = pltpu.make_async_copy(target, out, leave_sem.at[index])
        copy.start()
        leaving.append(copy)
    late[2].wait()

    total_wait(part_in.at[:, 0:1], sum_recv.at[0])
    group[0:1] = part[0:1] + jnp.sum(part_in[:, 0:1], axis=0)
    send_sums(group, group_in, second_peer, second_peers, 1)
    def inner(strip, carry):
        for index in range(2):
            rows_out[index, 0, strip] = tiles[index, strip * SH - 1]
            rows_out[index, 1, strip - 1] = tiles[index, strip * SH]
        return carry

    lax.fori_loop(1, strips, inner, 0)
    for copy in copies:
        copy.wait_recv()
    for index in range(2):
        for side in range(2):
            rows_out[index, side, side * (strips - 1)] = rows_in[side, index]
            cols_out[index, side, 1 : tile_rows + 1] = cols_in[side, index].astype(F32)
            above, below = corners_in[side, index], corners_in[2 + side, index]
            cols_out[index, side, 0:1] = above.astype(F32)[block - 1 : block]
            cols_out[index, side, tile_rows + 1 :] = jnp.broadcast_to(
                below.astype(F32)[0:1], (15, channels)
            )

    total_wait(group_in.at[:, 0:1], sum_recv.at[1])
    totals = group[0:1] + jnp.sum(group_in[:, 0:1], axis=0)
    totals_out[...] = jnp.broadcast_to(totals, (8, LANES)) / cell_count

    for copy in leaving:
        copy.wait()
    for copy in copies:
        copy.wait_send()
    total_wait(part_in.at[:, 0:1], sum_send.at[0])
    total_wait(group_in.at[:, 0:1], sum_send.at[1])


def margins(shape, stale_in, stale_hid, latent, weight_one, weight_two):
    tile_rows, tile_cols, channels = latent.shape
    n_row, n_col = shape
    strips = tile_rows // SH
    cell_count = float(tile_rows * tile_cols * n_row * n_col * (channels // GROUPS))
    hbm = pl.BlockSpec(memory_space=pltpu.HBM)
    vmem = pl.BlockSpec(memory_space=pltpu.VMEM)
    return pl.pallas_call(
        functools.partial(margins_kernel, cell_count, shape),
        out_shape=(
            jax.ShapeDtypeStruct((8, LANES), F32),
            jax.ShapeDtypeStruct((2, 2, strips, tile_cols, channels), BF16),
            jax.ShapeDtypeStruct((2, 2, tile_rows + 16, channels), F32),
            jax.ShapeDtypeStruct((tile_rows, tile_cols, channels), BF16),
            jax.ShapeDtypeStruct((4 * MAIN, 4 * MAIN), BF16),
            jax.ShapeDtypeStruct((4 * MAIN, 4 * MAIN), BF16),
        ),
        in_specs=[hbm] * 5,
        out_specs=(vmem,) * 4 + (hbm,) * 2,
        scratch_shapes=[
            pltpu.VMEM((2, tile_rows, tile_cols, channels), BF16),
            pltpu.VMEM((2, 4 * MAIN, 4 * MAIN), BF16),
            pltpu.VMEM((2,) + weight_one.shape, BF16),
            pltpu.VMEM((2, 2, tile_rows, channels), BF16),
            pltpu.VMEM((2, 2, tile_cols, channels), BF16),
            pltpu.VMEM((2, 2, tile_rows, channels), BF16),
            pltpu.VMEM((4, 2, 16, channels), BF16),
            pltpu.VMEM((8, LANES), F32),
            pltpu.VMEM((n_col // 2 - 1, 8, LANES), F32),
            pltpu.VMEM((8, LANES), F32),
            pltpu.VMEM((2 * n_row - 1, 8, LANES), F32),
            pltpu.SemaphoreType.DMA((2, 2)),
            pltpu.SemaphoreType.DMA((3,)),
            pltpu.SemaphoreType.DMA((2,)),
            pltpu.SemaphoreType.DMA((8,)),
            pltpu.SemaphoreType.DMA((8,)),
            pltpu.SemaphoreType.DMA((2,)),
            pltpu.SemaphoreType.DMA((2,)),
        ],
        compiler_params=pltpu.CompilerParams(
            collective_id=0, has_side_effects=True, vmem_limit_bytes=50 * 2**20
        ),
        name="margins",
    )(stale_in, stale_hid, latent, weight_one, weight_two)


def factors(totals, gains):
    channels = gains[0].shape[0]
    size = channels // GROUPS
    squares = pltpu.roll(totals, LANES - GROUPS, 1)
    lane_part = lax.div(lax.broadcasted_iota(jnp.int32, (8, LANES), 1), GROUPS)
    means = lax.rem(lane_part, 2) == 0
    spread = lax.rsqrt(jnp.where(means, squares - totals * totals, 1.0) + EPSILON)
    lead = lax.broadcasted_iota(jnp.int32, (8, LANES), 0) == 0
    packed = jnp.where(lead, totals, spread)
    groups = lax.broadcasted_iota(jnp.int32, (LANES, channels), 0)
    members = lax.broadcasted_iota(jnp.int32, (LANES, channels), 1)
    made = []
    for index, gain in enumerate(gains):
        own = (groups - 2 * GROUPS * index) * size
        valid = jnp.logical_and(groups >= 2 * GROUPS * index, groups < 2 * GROUPS * index + GROUPS)
        spill = one_hot(
            jnp.logical_and(valid, jnp.logical_and(members >= own, members < own + size))
        )
        spilt = jnp.dot(packed, spill, precision=EXACT, preferred_element_type=F32)
        made.append((spilt[0:1], spilt[1:2] * gain[...].reshape(1, channels) * 0.5))
    return made


def strips_kernel(
    shape,
    refresh,
    totals,
    gain_one,
    gain_two,
    rows,
    cols,
    shift,
    tile,
    far_first,
    far_second,
    far_hidden,
    block_out,
    hidden_out,
    first_weights,
    second_weights,
    stale_hid,
    edges,
    sides,
    hidden,
    finished,
    load_sem,
    store_sem,
):
    tile_rows, tile_cols, channels = tile.shape
    strips = tile_rows // SH
    cells = SH * tile_cols
    packs = cells // 8
    apart = tile_cols // 8
    loads = [
        pltpu.make_async_copy(far_first, first_weights, load_sem.at[0]),
        pltpu.make_async_copy(far_second, second_weights, load_sem.at[1]),
        pltpu.make_async_copy(far_hidden, stale_hid, load_sem.at[2]),
    ]
    for copy in loads:
        copy.start()
    weights = (first_weights, second_weights)
    n_row, n_col = shape
    row, col = lax.axis_index("row"), lax.axis_index("col")
    outside_rows = (row == 0, row == n_row - 1)
    outside_cols = (col == 0, col == n_col - 1)
    stats = factors(totals[...], (gain_one, gain_two))
    lines = lax.broadcasted_iota(jnp.int32, (cols.shape[2], 1), 0)
    beyond = jnp.logical_or(
        jnp.logical_and(lines == 0, outside_rows[0]),
        jnp.logical_and(lines == tile_rows + 1, outside_rows[1]),
    )
    for index in range(2):
        for side in range(2):
            value = act(cols[index, side], *stats[index])
            outside = jnp.logical_or(beyond, outside_cols[side])
            edges[index, side] = jnp.where(outside, 0.0, value)

    def margin_terms(index):
        for side in range(2):
            parts = [edges[index, side, a : a + tile_rows] for a in range(3)]
            lhs = side_by_side([part[:, :MAIN].astype(BF16) for part in parts], [tails(part) for part in parts])
            start = 2 * MAIN * side
            sides[index, side, :, :MAIN] = jnp.dot(
                lhs, weights[index][:, start : start + MAIN], preferred_element_type=F32
            )
            start = 3 * MAIN + LANES * side
            sides[index, side, :, MAIN:] = jnp.dot(
                lhs, weights[index][:, start : start + LANES], preferred_element_type=F32
            )
    sub = lax.broadcasted_iota(jnp.int32, (1, 8, 1), 1)

    def moved(index, side, strip, part, lanes):
        width = part.shape[-1]
        turned = pltpu.roll(part.reshape(packs, 8, width), 1 if side == 0 else 7, 1)
        pieces = []
        for line in range(SH):
            edge = jnp.broadcast_to(
                sides[index, side, strip * SH + line : strip * SH + line + 1, lanes], (8, width)
            )[None]
            first = line * apart
            if side == 0:
                pieces += [edge, turned[first : first + apart - 1]]
            else:
                pieces += [turned[first + 1 : first + apart], edge]
        carried = jnp.concatenate(pieces, axis=0)
        at = 0 if side == 0 else 7
        return jnp.where(sub == at, carried, turned).reshape(cells, width)

    def multiply(index, strip, inner):
        above, below = (
            act(rows[index, side, strip].astype(F32), *stats[index]) for side in range(2)
        )
        if strip == 0:
            above = jnp.where(outside_rows[0], 0.0, above)
        if strip == strips - 1:
            below = jnp.where(outside_rows[1], 0.0, below)
        values = jnp.concatenate([above[None], inner, below[None]], axis=0)
        main = values[..., :MAIN].astype(BF16)
        rest = tails(values)
        wide = side_by_side(
            [main[a : a + SH] for a in range(3)], [rest[a : a + SH] for a in range(3)]
        ).reshape(cells, 4 * MAIN)
        return [
            jnp.dot(
                wide,
                weights[index][:, part * MAIN : (part + 1) * MAIN],
                preferred_element_type=F32,
            )
            for part in range(4)
        ]

    def collect(index, strip, products):
        early, same, late, rest = products
        low, high = slice(0, MAIN), slice(MAIN, MAIN + LANES)
        main = moved(index, 0, strip, early, low) + same + moved(index, 1, strip, late, low)
        ends = (
            moved(index, 0, strip, rest[:, :LANES], high)
            + pltpu.roll(rest[:, :LANES], LANES // 2, 1)
            + moved(index, 1, strip, rest[:, LANES:], high)
        )
        return jnp.concatenate([main, ends[:, : channels - MAIN]], axis=1)

    fresh = {}

    def begin(index, strip):
        span = slice(strip * SH, strip * SH + SH)
        if index == 0:
            inner = act(tile[span].astype(F32), *stats[0])
        else:
            inner = act(fresh[strip].astype(F32), *stats[1])
        return multiply(index, strip, inner)

    def finish(index, strip, products):
        span = slice(strip * SH, strip * SH + SH)
        live = refresh[0, strip] > 0
        summed = collect(index, strip, products)
        if index == 0:
            value = (summed + shift[...].reshape(1, channels)).astype(BF16).reshape(SH, tile_cols, channels)
            fresh[strip] = value
            hidden[span] = jnp.where(live, value, stale_hid[span])
            made, out = hidden, hidden_out
        else:
            value = tile[span].astype(F32) + summed.reshape(SH, tile_cols, channels)
            finished[span] = jnp.where(live, value.astype(BF16), tile[span])
            made, out = finished, block_out
        pltpu.make_async_copy(made.at[span], out.at[span], store_sem.at[index]).start()

    loads[0].wait()
    margin_terms(0)
    jobs = [(index, strip) for half in range(0, strips, AHEAD) for index in range(2) for strip in range(half, half + AHEAD)]
    waiting, done = [], []
    for job in jobs:
        waiting.append((*job, begin(*job)))
        if len(waiting) > DEPTH:
            if len(done) == 0:
                for copy in loads[1:]:
                    copy.wait()
                margin_terms(1)
            done.append(waiting[0][:2])
            finish(*waiting.pop(0))
    for job in waiting:
        finish(*job)
    total_wait(hidden, store_sem.at[0])
    total_wait(finished, store_sem.at[1])


def refreshed(
    shape,
    refresh,
    totals,
    gain_one,
    gain_two,
    rows,
    cols,
    shift,
    tile,
    first_weights,
    second_weights,
    stale_hid,
):
    tile_shape = tile.shape
    tile_rows, tile_cols, channels = tile_shape
    anywhere = pl.BlockSpec(memory_space=pl.ANY)
    vmem = pl.BlockSpec(memory_space=pltpu.VMEM)
    out = jax.ShapeDtypeStruct(tile_shape, BF16)
    return pl.pallas_call(
        functools.partial(strips_kernel, shape),
        out_shape=(out, out),
        in_specs=[pl.BlockSpec(memory_space=pltpu.SMEM)] + [vmem] * 7 + [anywhere] * 3,
        out_specs=(anywhere, anywhere),
        scratch_shapes=[
            pltpu.VMEM((4 * MAIN, 4 * MAIN), BF16),
            pltpu.VMEM((4 * MAIN, 4 * MAIN), BF16),
            pltpu.VMEM(tile_shape, BF16),
            pltpu.VMEM(cols.shape, F32),
            pltpu.VMEM((2, 2, tile_rows, MAIN + LANES), F32),
            pltpu.VMEM(tile_shape, BF16),
            pltpu.VMEM(tile_shape, BF16),
            pltpu.SemaphoreType.DMA((3,)),
            pltpu.SemaphoreType.DMA((2,)),
        ],
        compiler_params=pltpu.CompilerParams(vmem_limit_bytes=50 * 2**20),
        name="strips",
    )(
        refresh,
        totals,
        gain_one,
        gain_two,
        rows,
        cols,
        shift,
        tile,
        first_weights,
        second_weights,
        stale_hid,
    )


def per_device(
    shape,
    latent,
    stale_input,
    stale_hidden,
    refresh,
    gain_one,
    weight_one,
    time_shift,
    gain_two,
    weight_two,
):
    totals, rows, cols, tile, first_weights, second_weights = margins(
        shape, stale_input, stale_hidden, latent, weight_one, weight_two
    )
    return refreshed(
        shape,
        refresh.T,
        totals,
        gain_one,
        gain_two,
        rows,
        cols,
        time_shift,
        tile,
        first_weights,
        second_weights,
        stale_hidden,
    )


def solution(mesh):
    placed = (
        P("row", "col", None),
        P("row", "col", None),
        P("row", "col", None),
        P("row", "col"),
        P(),
        P(),
        P(),
        P(),
        P(),
    )
    return jax.shard_map(
        functools.partial(per_device, (mesh.shape["row"], mesh.shape["col"])),
        mesh=mesh,
        in_specs=placed,
        out_specs=(P("row", "col", None), P("row", "col", None)),
        check_vma=False,
    )
```

```python
import functools

import jax
import jax.numpy as jnp
from jax import lax
from jax.experimental import pallas as pl
from jax.experimental.pallas import tpu as pltpu
from jax.sharding import PartitionSpec as P

GROUPS = 32
SH = 8
EPSILON = 1e-05
LANES = 128
EXACT = lax.Precision.HIGHEST
F32 = jnp.float32
BF16 = jnp.bfloat16
MAIN = 256


def act(values, center, half_scale):
    half = (values - center) * half_scale
    return half * jnp.tanh(half) + half


def one_hot(condition, kind=F32):
    return jnp.where(condition, 1.0, 0.0).astype(kind)


def total_wait(buffer, semaphore):
    pltpu.make_async_copy(buffer, buffer, semaphore).wait()


def tails(values):
    rest = values[..., MAIN:]
    blank = jnp.zeros(rest.shape[:-1] + (LANES - rest.shape[-1],), rest.dtype)
    return jnp.concatenate([rest, blank], axis=-1)


def side_by_side(main, rest):
    turned = pltpu.roll(rest[1], LANES // 2, rest[1].ndim - 1)
    pairs = (rest[0] + turned).astype(BF16)
    return jnp.concatenate([*main, pairs, rest[2].astype(BF16)], axis=-1)


def margins_kernel(
    cell_count,
    shape,
    stale_in,
    stale_hid,
    latent,
    weight_one,
    weight_two,
    totals_out,
    rows_out,
    cols_out,
    tile_out,
    first_weights,
    second_weights,
    tiles,
    laid_out,
    raw,
    cols,
    rows_in,
    cols_in,
    corners_in,
    part,
    part_in,
    group,
    group_in,
    load_sem,
    late_sem,
    leave_sem,
    side_send,
    side_recv,
    sum_send,
    sum_recv,
):
    n_row, n_col = shape
    row, col = lax.axis_index("row"), lax.axis_index("col")
    tile_rows, tile_cols, channels = tiles.shape[1:]
    strips = tile_rows // SH
    up, down = lax.rem(row + n_row - 1, n_row), lax.rem(row + 1, n_row)
    left, right = lax.rem(col + n_col - 1, n_col), lax.rem(col + 1, n_col)
    core, x_high, z = lax.rem(col, 2), lax.rem(lax.div(col, 2), 2), lax.div(col, 4)
    y, x = lax.rem(row, 4), x_high * 2 + lax.div(row, 4)
    deep = n_col // 4
    first_peers, second_peers = 2 * deep - 1, 2 * n_row - 1

    def first_peer(step):
        place = lax.rem(z * 2 + core + lax.rem(step + deep - 1, first_peers) + 1, 2 * deep)
        return row, lax.div(place, 2) * 4 + x_high * 2 + lax.rem(place, 2)

    def second_peer(step):
        offset = lax.rem(step + 9, second_peers) + 1
        there_x, there_y = lax.rem(x + lax.div(offset, 4), 4), lax.rem(y + lax.rem(offset, 4), 4)
        there_row = lax.rem(there_x, 2) * 4 + there_y
        return there_row, z * 4 + lax.div(there_x, 2) * 2 + core

    def signal(device):
        pl.semaphore_signal(
            barrier, inc=1, device_id=device, device_id_type=pl.DeviceIdType.MESH
        )

    loads = []
    half = tile_rows // 2
    for index, source in enumerate((stale_in, stale_hid)):
        for piece in range(2):
            span = pl.ds(piece * half, half)
            copy = pltpu.make_async_copy(
                source.at[span], tiles.at[index, span], load_sem.at[index, piece]
            )
            copy.start()
            loads.append(copy)

    late = [
        pltpu.make_async_copy(weight_one, raw.at[0], late_sem.at[0]),
        pltpu.make_async_copy(weight_two, raw.at[1], late_sem.at[1]),
        pltpu.make_async_copy(latent, tile_out, late_sem.at[2]),
    ]
    for copy in late:
        copy.start()

    barrier = pltpu.get_barrier_semaphore()

    @pl.loop(0, first_peers)
    def _(step):
        signal(first_peer(step))
        signal(second_peer(step))

    for place in (up, row, down):
        for device in ((place, left), (place, right)):
            signal(device)
    signal((up, col))
    signal((down, col))

    lines = lax.broadcasted_iota(jnp.int32, (channels, LANES), 0)
    lanes = lax.rem(lax.broadcasted_iota(jnp.int32, (channels, LANES), 1), GROUPS)
    size = channels // GROUPS
    gather = one_hot(jnp.logical_and(lines >= lanes * size, lines < lanes * size + size))
    sums = []
    for index in range(2):
        zero = jnp.zeros((tile_cols, channels), F32)
        carry = (zero, zero)
        for piece in range(2):
            loads[2 * index + piece].wait()

            def add(line, carry):
                values = tiles[index, line].astype(F32)
                return carry[0] + values, carry[1] + values * values

            carry = lax.fori_loop(piece * half, (piece + 1) * half, add, carry, unroll=4)
        sums += [jnp.sum(carry[0], axis=0, keepdims=True), jnp.sum(carry[1], axis=0, keepdims=True)]
    stacked = jnp.concatenate(sums + [jnp.zeros((4, channels), F32)], axis=0)
    grouped = jnp.dot(stacked, gather, precision=EXACT, preferred_element_type=F32)
    lane_part = lax.div(lax.broadcasted_iota(jnp.int32, (8, LANES), 1), GROUPS)
    kept = jnp.where(lane_part == lax.broadcasted_iota(jnp.int32, (8, LANES), 0), grouped, 0.0)
    part[...] = jnp.broadcast_to(jnp.sum(kept, axis=0, keepdims=True), (8, LANES))

    pl.semaphore_wait(barrier, first_peers + second_peers + 8)

    def send_sums(source, target, peer, count, phase):
        @pl.loop(0, count)
        def _(step):
            pltpu.make_async_remote_copy(
                src_ref=source.at[0:1],
                dst_ref=target.at[step, 0:1],
                send_sem=sum_send.at[phase],
                recv_sem=sum_recv.at[phase],
                device_id=peer(step),
                device_id_type=pl.DeviceIdType.MESH,
            ).start()

    send_sums(part, part_in, first_peer, first_peers, 0)

    block = 16
    picks = lax.broadcasted_iota(jnp.int32, (2 * block, block * tile_cols), 0)
    cells = lax.broadcasted_iota(jnp.int32, (2 * block, block * tile_cols), 1)
    wanted = jnp.where(picks < block, picks * tile_cols, (picks - block) * tile_cols + tile_cols - 1)
    select = one_hot(cells == wanted, BF16)
    for index in range(2):
        for piece in range(tile_rows // block):
            span = pl.ds(piece * block, block)
            flat = tiles[index, span].reshape(block * tile_cols, channels)
            picked = jnp.dot(select, flat, preferred_element_type=F32).astype(BF16)
            cols[0, index, span] = picked[:block]
            cols[1, index, span] = picked[block:]

    head, tail = pl.ds(0, block), pl.ds(tile_rows - block, block)
    every = slice(None)
    moves = (
        (tiles.at[:, 0], rows_in.at[1], (up, col)),
        (tiles.at[:, tile_rows - 1], rows_in.at[0], (down, col)),
        (cols.at[0], cols_in.at[1], (row, left)),
        (cols.at[1], cols_in.at[0], (row, right)),
        (cols.at[0, every, head], corners_in.at[3], (up, left)),
        (cols.at[1, every, head], corners_in.at[2], (up, right)),
        (cols.at[0, every, tail], corners_in.at[1], (down, left)),
        (cols.at[1, every, tail], corners_in.at[0], (down, right)),
    )
    copies = []
    for index, (source, target, device) in enumerate(moves):
        copy = pltpu.make_async_remote_copy(
            src_ref=source,
            dst_ref=target,
            send_sem=side_send.at[index],
            recv_sem=side_recv.at[index],
            device_id=device,
            device_id_type=pl.DeviceIdType.MESH,
        )
        copy.start()
        copies.append(copy)

    leaving = []
    for index in range(2):
        late[index].wait()
        target = laid_out.at[index]
        for down_tap in range(3):
            taps = [raw[index, 3 * down_tap + across] for across in range(3)]
            rest = [tap[:, MAIN:] for tap in taps]
            blank = jnp.zeros_like(rest[0])
            ends = jnp.concatenate(rest + [blank], axis=1)
            pieces = [tap[:, :MAIN] for tap in taps] + [ends]
            for place, piece in enumerate(pieces):
                lanes = pl.ds(place * MAIN, MAIN)
                target[pl.ds(down_tap * MAIN, MAIN), lanes] = piece[:MAIN]
                spot = pl.ds(3 * MAIN + down_tap * (channels - MAIN), channels - MAIN)
                target[spot, lanes] = piece[MAIN:]
        spot = pl.ds(3 * channels, 4 * MAIN - 3 * channels)
        target[spot] = jnp.zeros((4 * MAIN - 3 * channels, 4 * MAIN), BF16)
        out = (first_weights, second_weights)[index]
        copy = pltpu.make_async_copy(target, out, leave_sem.at[index])
        copy.start()
        leaving.append(copy)
    late[2].wait()

    total_wait(part_in.at[:, 0:1], sum_recv.at[0])
    group[0:1] = part[0:1] + jnp.sum(part_in[:, 0:1], axis=0)
    send_sums(group, group_in, second_peer, second_peers, 1)
    def inner(strip, carry):
        for index in range(2):
            rows_out[index, 0, strip] = tiles[index, strip * SH - 1]
            rows_out[index, 1, strip - 1] = tiles[index, strip * SH]
        return carry

    lax.fori_loop(1, strips, inner, 0)
    for copy in copies:
        copy.wait_recv()
    for index in range(2):
        for side in range(2):
            rows_out[index, side, side * (strips - 1)] = rows_in[side, index]
            cols_out[index, side, 1 : tile_rows + 1] = cols_in[side, index].astype(F32)
            above, below = corners_in[side, index], corners_in[2 + side, index]
            cols_out[index, side, 0:1] = above.astype(F32)[block - 1 : block]
            cols_out[index, side, tile_rows + 1 :] = jnp.broadcast_to(
                below.astype(F32)[0:1], (15, channels)
            )

    total_wait(group_in.at[:, 0:1], sum_recv.at[1])
    totals = group[0:1] + jnp.sum(group_in[:, 0:1], axis=0)
    totals_out[...] = jnp.broadcast_to(totals, (8, LANES)) / cell_count

    for copy in leaving:
        copy.wait()
    for copy in copies:
        copy.wait_send()
    total_wait(part_in.at[:, 0:1], sum_send.at[0])
    total_wait(group_in.at[:, 0:1], sum_send.at[1])


def margins(shape, stale_in, stale_hid, latent, weight_one, weight_two):
    tile_rows, tile_cols, channels = latent.shape
    n_row, n_col = shape
    strips = tile_rows // SH
    cell_count = float(tile_rows * tile_cols * n_row * n_col * (channels // GROUPS))
    hbm = pl.BlockSpec(memory_space=pltpu.HBM)
    vmem = pl.BlockSpec(memory_space=pltpu.VMEM)
    return pl.pallas_call(
        functools.partial(margins_kernel, cell_count, shape),
        out_shape=(
            jax.ShapeDtypeStruct((8, LANES), F32),
            jax.ShapeDtypeStruct((2, 2, strips, tile_cols, channels), BF16),
            jax.ShapeDtypeStruct((2, 2, tile_rows + 16, channels), F32),
            jax.ShapeDtypeStruct((tile_rows, tile_cols, channels), BF16),
            jax.ShapeDtypeStruct((4 * MAIN, 4 * MAIN), BF16),
            jax.ShapeDtypeStruct((4 * MAIN, 4 * MAIN), BF16),
        ),
        in_specs=[hbm] * 5,
        out_specs=(vmem,) * 4 + (hbm,) * 2,
        scratch_shapes=[
            pltpu.VMEM((2, tile_rows, tile_cols, channels), BF16),
            pltpu.VMEM((2, 4 * MAIN, 4 * MAIN), BF16),
            pltpu.VMEM((2,) + weight_one.shape, BF16),
            pltpu.VMEM((2, 2, tile_rows, channels), BF16),
            pltpu.VMEM((2, 2, tile_cols, channels), BF16),
            pltpu.VMEM((2, 2, tile_rows, channels), BF16),
            pltpu.VMEM((4, 2, 16, channels), BF16),
            pltpu.VMEM((8, LANES), F32),
            pltpu.VMEM((n_col // 2 - 1, 8, LANES), F32),
            pltpu.VMEM((8, LANES), F32),
            pltpu.VMEM((2 * n_row - 1, 8, LANES), F32),
            pltpu.SemaphoreType.DMA((2, 2)),
            pltpu.SemaphoreType.DMA((3,)),
            pltpu.SemaphoreType.DMA((2,)),
            pltpu.SemaphoreType.DMA((8,)),
            pltpu.SemaphoreType.DMA((8,)),
            pltpu.SemaphoreType.DMA((2,)),
            pltpu.SemaphoreType.DMA((2,)),
        ],
        compiler_params=pltpu.CompilerParams(
            collective_id=0, has_side_effects=True, vmem_limit_bytes=50 * 2**20
        ),
        name="margins",
    )(stale_in, stale_hid, latent, weight_one, weight_two)


def factors(totals, gains):
    channels = gains[0].shape[0]
    size = channels // GROUPS
    squares = pltpu.roll(totals, LANES - GROUPS, 1)
    lane_part = lax.div(lax.broadcasted_iota(jnp.int32, (8, LANES), 1), GROUPS)
    means = lax.rem(lane_part, 2) == 0
    spread = lax.rsqrt(jnp.where(means, squares - totals * totals, 1.0) + EPSILON)
    groups = lax.broadcasted_iota(jnp.int32, (LANES, channels), 0)
    members = lax.broadcasted_iota(jnp.int32, (LANES, channels), 1)
    parts = []
    for value in (totals[0:1], spread[0:1]):
        for _ in range(3):
            parts.append(value.astype(BF16).astype(F32))
            value = value - parts[-1]
    packed = jnp.concatenate(parts + [jnp.zeros((2, LANES), F32)], axis=0).astype(BF16)
    made = []
    for index, gain in enumerate(gains):
        own = (groups - 2 * GROUPS * index) * size
        valid = jnp.logical_and(groups >= 2 * GROUPS * index, groups < 2 * GROUPS * index + GROUPS)
        spill = one_hot(
            jnp.logical_and(valid, jnp.logical_and(members >= own, members < own + size)), BF16
        )
        spilt = jnp.dot(packed, spill, preferred_element_type=F32)
        center = spilt[0:1] + spilt[1:2] + spilt[2:3]
        scale = spilt[3:4] + spilt[4:5] + spilt[5:6]
        made.append((center, scale * gain[...].reshape(1, channels) * 0.5))
    return made


def strips_kernel(
    shape,
    refresh,
    totals,
    gain_one,
    gain_two,
    rows,
    cols,
    shift,
    tile,
    far_first,
    far_second,
    far_hidden,
    block_out,
    hidden_out,
    first_weights,
    second_weights,
    stale_hid,
    order,
    edges,
    sides,
    hidden,
    finished,
    load_sem,
    store_sem,
):
    tile_rows, tile_cols, channels = tile.shape
    strips = tile_rows // SH
    cells = SH * tile_cols
    packs = cells // 8
    apart = tile_cols // 8
    loads = [
        pltpu.make_async_copy(far_first, first_weights, load_sem.at[0]),
        pltpu.make_async_copy(far_second, second_weights, load_sem.at[1]),
        pltpu.make_async_copy(far_hidden, stale_hid, load_sem.at[2]),
    ]
    for copy in loads:
        copy.start()
    weights = (first_weights, second_weights)
    live_total = sum(refresh[0, strip] for strip in range(strips))
    pairs = lax.div(live_total + 1, 2)
    before = jnp.int32(0)
    for strip in range(strips):
        flag = refresh[0, strip]
        order[jnp.where(flag > 0, before, live_total + strip - before)] = jnp.int32(strip)
        before += flag
    for place in range(strips):

        @pl.when(place >= 2 * pairs)
        def _():
            span = pl.ds(order[place] * SH, SH)
            pltpu.make_async_copy(far_hidden.at[span], hidden_out.at[span], store_sem.at[0]).start()
            pltpu.make_async_copy(tile.at[span], block_out.at[span], store_sem.at[1]).start()

    n_row, n_col = shape
    row, col = lax.axis_index("row"), lax.axis_index("col")
    outside_rows = (row == 0, row == n_row - 1)
    outside_cols = (col == 0, col == n_col - 1)
    stats = factors(totals[...], (gain_one, gain_two))
    lines = lax.broadcasted_iota(jnp.int32, (cols.shape[2], 1), 0)
    beyond = jnp.logical_or(
        jnp.logical_and(lines == 0, outside_rows[0]),
        jnp.logical_and(lines == tile_rows + 1, outside_rows[1]),
    )
    for index in range(2):
        for side in range(2):
            value = act(cols[index, side], *stats[index])
            outside = jnp.logical_or(beyond, outside_cols[side])
            edges[index, side] = jnp.where(outside, 0.0, value)

    def margin_terms(index):
        for side in range(2):
            parts = [edges[index, side, a : a + tile_rows] for a in range(3)]
            lhs = side_by_side([part[:, :MAIN].astype(BF16) for part in parts], [tails(part) for part in parts])
            start = 2 * MAIN * side
            sides[index, side, :, :MAIN] = jnp.dot(
                lhs, weights[index][:, start : start + MAIN], preferred_element_type=F32
            )
            start = 3 * MAIN + LANES * side
            sides[index, side, :, MAIN:] = jnp.dot(
                lhs, weights[index][:, start : start + LANES], preferred_element_type=F32
            )
    sub = lax.broadcasted_iota(jnp.int32, (1, 8, 1), 1)

    def moved(index, side, strip, part, lanes):
        width = part.shape[-1]
        turned = pltpu.roll(part.reshape(packs, 8, width), 1 if side == 0 else 7, 1)
        pieces = []
        margin = sides[index, side, pl.ds(pl.multiple_of(strip * SH, SH), SH), lanes]
        for line in range(SH):
            edge = jnp.broadcast_to(margin[line : line + 1], (8, width))[None]
            first = line * apart
            if side == 0:
                pieces += [edge, turned[first : first + apart - 1]]
            else:
                pieces += [turned[first + 1 : first + apart], edge]
        carried = jnp.concatenate(pieces, axis=0)
        at = 0 if side == 0 else 7
        return jnp.where(sub == at, carried, turned).reshape(cells, width)

    def multiply(index, strip, inner):
        above, below = (
            act(rows[index, side, strip].astype(F32), *stats[index]) for side in range(2)
        )
        above = jnp.where(jnp.logical_and(strip == 0, outside_rows[0]), 0.0, above)
        below = jnp.where(jnp.logical_and(strip == strips - 1, outside_rows[1]), 0.0, below)
        values = jnp.concatenate([above[None], inner, below[None]], axis=0)
        main = values[..., :MAIN].astype(BF16)
        rest = tails(values)
        wide = side_by_side(
            [main[a : a + SH] for a in range(3)], [rest[a : a + SH] for a in range(3)]
        ).reshape(cells, 4 * MAIN)
        return [
            jnp.dot(
                wide,
                weights[index][:, part * MAIN : (part + 1) * MAIN],
                preferred_element_type=F32,
            )
            for part in range(4)
        ]

    def collect(index, strip, products):
        early, same, late, rest = products
        low, high = slice(0, MAIN), slice(MAIN, MAIN + LANES)
        main = moved(index, 0, strip, early, low) + same + moved(index, 1, strip, late, low)
        ends = (
            moved(index, 0, strip, rest[:, :LANES], high)
            + pltpu.roll(rest[:, :LANES], LANES // 2, 1)
            + moved(index, 1, strip, rest[:, LANES:], high)
        )
        return jnp.concatenate([main, ends[:, : channels - MAIN]], axis=1)

    loads[0].wait()
    margin_terms(0)
    for copy in loads[1:]:
        copy.wait()
    margin_terms(1)

    def one_pair(pair, carry):
        places = [order[2 * pair + local] for local in range(2)]
        spans = [pl.ds(strip * SH, SH) for strip in places]
        lives = [refresh[0, strip] > 0 for strip in places]
        fresh = [None, None]

        def begin(index, local):
            if index == 0:
                inner = act(tile[spans[local]].astype(F32), *stats[0])
            else:
                inner = act(fresh[local].astype(F32), *stats[1])
            return multiply(index, places[local], inner)

        def finish(index, local, products):
            span, live = spans[local], lives[local]
            summed = collect(index, places[local], products)
            if index == 0:
                value = (summed + shift[...].reshape(1, channels)).astype(BF16)
                fresh[local] = value.reshape(SH, tile_cols, channels)
                hidden[span] = jnp.where(live, fresh[local], stale_hid[span])
                made, out = hidden, hidden_out
            else:
                value = tile[span].astype(F32) + summed.reshape(SH, tile_cols, channels)
                finished[span] = jnp.where(live, value.astype(BF16), tile[span])
                made, out = finished, block_out
            pltpu.make_async_copy(made.at[span], out.at[span], store_sem.at[index]).start()

        waiting = None
        for index, local in ((0, 0), (0, 1), (1, 0), (1, 1)):
            products = begin(index, local)
            if waiting is not None:
                finish(*waiting)
            waiting = (index, local, products)
        finish(*waiting)
        return carry

    lax.fori_loop(0, pairs, one_pair, 0)
    total_wait(hidden, store_sem.at[0])
    total_wait(finished, store_sem.at[1])


def refreshed(
    shape,
    refresh,
    totals,
    gain_one,
    gain_two,
    rows,
    cols,
    shift,
    tile,
    first_weights,
    second_weights,
    stale_hid,
):
    tile_shape = tile.shape
    tile_rows, tile_cols, channels = tile_shape
    strip_total = tile_rows // SH
    anywhere = pl.BlockSpec(memory_space=pl.ANY)
    vmem = pl.BlockSpec(memory_space=pltpu.VMEM)
    out = jax.ShapeDtypeStruct(tile_shape, BF16)
    return pl.pallas_call(
        functools.partial(strips_kernel, shape),
        out_shape=(out, out),
        in_specs=[pl.BlockSpec(memory_space=pltpu.SMEM)] + [vmem] * 7 + [anywhere] * 3,
        out_specs=(anywhere, anywhere),
        scratch_shapes=[
            pltpu.VMEM((4 * MAIN, 4 * MAIN), BF16),
            pltpu.VMEM((4 * MAIN, 4 * MAIN), BF16),
            pltpu.VMEM(tile_shape, BF16),
            pltpu.SMEM((strip_total,), jnp.int32),
            pltpu.VMEM(cols.shape, F32),
            pltpu.VMEM((2, 2, tile_rows, MAIN + LANES), F32),
            pltpu.VMEM(tile_shape, BF16),
            pltpu.VMEM(tile_shape, BF16),
            pltpu.SemaphoreType.DMA((3,)),
            pltpu.SemaphoreType.DMA((2,)),
        ],
        compiler_params=pltpu.CompilerParams(vmem_limit_bytes=50 * 2**20),
        name="strips",
    )(
        refresh,
        totals,
        gain_one,
        gain_two,
        rows,
        cols,
        shift,
        tile,
        first_weights,
        second_weights,
        stale_hid,
    )


def per_device(
    shape,
    latent,
    stale_input,
    stale_hidden,
    refresh,
    gain_one,
    weight_one,
    time_shift,
    gain_two,
    weight_two,
):
    totals, rows, cols, tile, first_weights, second_weights = margins(
        shape, stale_input, stale_hidden, latent, weight_one, weight_two
    )
    return refreshed(
        shape,
        refresh.T,
        totals,
        gain_one,
        gain_two,
        rows,
        cols,
        time_shift,
        tile,
        first_weights,
        second_weights,
        stale_hidden,
    )


def solution(mesh):
    placed = (
        P("row", "col", None),
        P("row", "col", None),
        P("row", "col", None),
        P("row", "col"),
        P(),
        P(),
        P(),
        P(),
        P(),
    )
    return jax.shard_map(
        functools.partial(per_device, (mesh.shape["row"], mesh.shape["col"])),
        mesh=mesh,
        in_specs=placed,
        out_specs=(P("row", "col", None), P("row", "col", None)),
        check_vma=False,
    )
```

```python
import functools

import jax
import jax.numpy as jnp
from jax import lax
from jax.experimental import pallas as pl
from jax.experimental.pallas import tpu as pltpu
from jax.sharding import PartitionSpec as P

GROUPS = 32
SH = 8
EPSILON = 1e-05
LANES = 128
EXACT = lax.Precision.HIGHEST
F32 = jnp.float32
BF16 = jnp.bfloat16
MAIN = 256


def act(values, center, half_scale):
    half = (values - center) * half_scale
    return half * jnp.tanh(half) + half


def one_hot(condition, kind=F32):
    return jnp.where(condition, 1.0, 0.0).astype(kind)


def total_wait(buffer, semaphore):
    pltpu.make_async_copy(buffer, buffer, semaphore).wait()


def tails(values):
    rest = values[..., MAIN:]
    blank = jnp.zeros(rest.shape[:-1] + (LANES - rest.shape[-1],), rest.dtype)
    return jnp.concatenate([rest, blank], axis=-1)


def side_by_side(main, rest):
    turned = pltpu.roll(rest[1], LANES // 2, rest[1].ndim - 1)
    pairs = (rest[0] + turned).astype(BF16)
    return jnp.concatenate([*main, pairs, rest[2].astype(BF16)], axis=-1)


def margins_kernel(
    cell_count,
    shape,
    stale_in,
    stale_hid,
    latent,
    weight_one,
    weight_two,
    totals_out,
    rows_out,
    cols_out,
    tile_out,
    first_weights,
    second_weights,
    tiles,
    laid_out,
    raw,
    cols,
    rows_in,
    cols_in,
    corners_in,
    part,
    part_in,
    group,
    group_in,
    load_sem,
    late_sem,
    leave_sem,
    side_send,
    side_recv,
    sum_send,
    sum_recv,
):
    n_row, n_col = shape
    row, col = lax.axis_index("row"), lax.axis_index("col")
    tile_rows, tile_cols, channels = tiles.shape[1:]
    strips = tile_rows // SH
    up, down = lax.rem(row + n_row - 1, n_row), lax.rem(row + 1, n_row)
    left, right = lax.rem(col + n_col - 1, n_col), lax.rem(col + 1, n_col)
    core, x_high, z = lax.rem(col, 2), lax.rem(lax.div(col, 2), 2), lax.div(col, 4)
    y, x = lax.rem(row, 4), x_high * 2 + lax.div(row, 4)
    deep = n_col // 4
    first_peers, second_peers = 2 * deep - 1, 2 * n_row - 1

    def first_peer(step):
        place = lax.rem(z * 2 + core + lax.rem(step + deep - 1, first_peers) + 1, 2 * deep)
        return row, lax.div(place, 2) * 4 + x_high * 2 + lax.rem(place, 2)

    def second_peer(step):
        offset = lax.rem(step + 9, second_peers) + 1
        there_x, there_y = lax.rem(x + lax.div(offset, 4), 4), lax.rem(y + lax.rem(offset, 4), 4)
        there_row = lax.rem(there_x, 2) * 4 + there_y
        return there_row, z * 4 + lax.div(there_x, 2) * 2 + core

    def signal(device):
        pl.semaphore_signal(
            barrier, inc=1, device_id=device, device_id_type=pl.DeviceIdType.MESH
        )

    loads = []
    half = tile_rows // 2
    for index, source in enumerate((stale_in, stale_hid)):
        for piece in range(2):
            span = pl.ds(piece * half, half)
            copy = pltpu.make_async_copy(
                source.at[span], tiles.at[index, span], load_sem.at[index, piece]
            )
            copy.start()
            loads.append(copy)

    late = [
        pltpu.make_async_copy(weight_one, raw.at[0], late_sem.at[0]),
        pltpu.make_async_copy(weight_two, raw.at[1], late_sem.at[1]),
        pltpu.make_async_copy(latent, tile_out, late_sem.at[2]),
    ]
    for copy in late:
        copy.start()

    barrier = pltpu.get_barrier_semaphore()

    @pl.loop(0, first_peers)
    def _(step):
        signal(first_peer(step))
        signal(second_peer(step))

    for place in (up, row, down):
        for device in ((place, left), (place, right)):
            signal(device)
    signal((up, col))
    signal((down, col))

    lines = lax.broadcasted_iota(jnp.int32, (channels, LANES), 0)
    lanes = lax.rem(lax.broadcasted_iota(jnp.int32, (channels, LANES), 1), GROUPS)
    size = channels // GROUPS
    gather = one_hot(jnp.logical_and(lines >= lanes * size, lines < lanes * size + size))
    sums = []
    for index in range(2):
        zero = jnp.zeros((tile_cols, channels), F32)
        carry = (zero, zero)
        for piece in range(2):
            loads[2 * index + piece].wait()

            def add(line, carry):
                values = tiles[index, line].astype(F32)
                return carry[0] + values, carry[1] + values * values

            carry = lax.fori_loop(piece * half, (piece + 1) * half, add, carry, unroll=4)
        sums += [jnp.sum(carry[0], axis=0, keepdims=True), jnp.sum(carry[1], axis=0, keepdims=True)]
    stacked = jnp.concatenate(sums + [jnp.zeros((4, channels), F32)], axis=0)
    grouped = jnp.dot(stacked, gather, precision=EXACT, preferred_element_type=F32)
    lane_part = lax.div(lax.broadcasted_iota(jnp.int32, (8, LANES), 1), GROUPS)
    kept = jnp.where(lane_part == lax.broadcasted_iota(jnp.int32, (8, LANES), 0), grouped, 0.0)
    part[...] = jnp.broadcast_to(jnp.sum(kept, axis=0, keepdims=True), (8, LANES))

    pl.semaphore_wait(barrier, first_peers + second_peers + 8)

    def send_sums(source, target, peer, count, phase):
        @pl.loop(0, count)
        def _(step):
            pltpu.make_async_remote_copy(
                src_ref=source.at[0:1],
                dst_ref=target.at[step, 0:1],
                send_sem=sum_send.at[phase],
                recv_sem=sum_recv.at[phase],
                device_id=peer(step),
                device_id_type=pl.DeviceIdType.MESH,
            ).start()

    send_sums(part, part_in, first_peer, first_peers, 0)

    block = 16
    picks = lax.broadcasted_iota(jnp.int32, (2 * block, block * tile_cols), 0)
    cells = lax.broadcasted_iota(jnp.int32, (2 * block, block * tile_cols), 1)
    wanted = jnp.where(picks < block, picks * tile_cols, (picks - block) * tile_cols + tile_cols - 1)
    select = one_hot(cells == wanted, BF16)
    for index in range(2):
        for piece in range(tile_rows // block):
            span = pl.ds(piece * block, block)
            flat = tiles[index, span].reshape(block * tile_cols, channels)
            picked = jnp.dot(select, flat, preferred_element_type=F32).astype(BF16)
            cols[0, index, span] = picked[:block]
            cols[1, index, span] = picked[block:]

    head, tail = pl.ds(0, block), pl.ds(tile_rows - block, block)
    every = slice(None)
    moves = (
        (tiles.at[:, 0], rows_in.at[1], (up, col)),
        (tiles.at[:, tile_rows - 1], rows_in.at[0], (down, col)),
        (cols.at[0], cols_in.at[1], (row, left)),
        (cols.at[1], cols_in.at[0], (row, right)),
        (cols.at[0, every, head], corners_in.at[3], (up, left)),
        (cols.at[1, every, head], corners_in.at[2], (up, right)),
        (cols.at[0, every, tail], corners_in.at[1], (down, left)),
        (cols.at[1, every, tail], corners_in.at[0], (down, right)),
    )
    copies = []
    for index, (source, target, device) in enumerate(moves):
        copy = pltpu.make_async_remote_copy(
            src_ref=source,
            dst_ref=target,
            send_sem=side_send.at[index],
            recv_sem=side_recv.at[index],
            device_id=device,
            device_id_type=pl.DeviceIdType.MESH,
        )
        copy.start()
        copies.append(copy)

    leaving = []
    for index in range(2):
        late[index].wait()
        target = laid_out.at[index]
        for down_tap in range(3):
            taps = [raw[index, 3 * down_tap + across] for across in range(3)]
            rest = [tap[:, MAIN:] for tap in taps]
            blank = jnp.zeros_like(rest[0])
            ends = jnp.concatenate(rest + [blank], axis=1)
            pieces = [tap[:, :MAIN] for tap in taps] + [ends]
            for place, piece in enumerate(pieces):
                lanes = pl.ds(place * MAIN, MAIN)
                target[pl.ds(down_tap * MAIN, MAIN), lanes] = piece[:MAIN]
                spot = pl.ds(3 * MAIN + down_tap * (channels - MAIN), channels - MAIN)
                target[spot, lanes] = piece[MAIN:]
        spot = pl.ds(3 * channels, 4 * MAIN - 3 * channels)
        target[spot] = jnp.zeros((4 * MAIN - 3 * channels, 4 * MAIN), BF16)
        out = (first_weights, second_weights)[index]
        copy = pltpu.make_async_copy(target, out, leave_sem.at[index])
        copy.start()
        leaving.append(copy)
    late[2].wait()

    total_wait(part_in.at[:, 0:1], sum_recv.at[0])
    group[0:1] = part[0:1] + jnp.sum(part_in[:, 0:1], axis=0)
    send_sums(group, group_in, second_peer, second_peers, 1)
    def inner(strip, carry):
        for index in range(2):
            rows_out[index, 0, strip] = tiles[index, strip * SH - 1]
            rows_out[index, 1, strip - 1] = tiles[index, strip * SH]
        return carry

    lax.fori_loop(1, strips, inner, 0)
    for copy in copies:
        copy.wait_recv()
    for index in range(2):
        for side in range(2):
            rows_out[index, side, side * (strips - 1)] = rows_in[side, index]
            cols_out[index, side, 1 : tile_rows + 1] = cols_in[side, index].astype(F32)
            above, below = corners_in[side, index], corners_in[2 + side, index]
            cols_out[index, side, 0:1] = above.astype(F32)[block - 1 : block]
            cols_out[index, side, tile_rows + 1 :] = jnp.broadcast_to(
                below.astype(F32)[0:1], (15, channels)
            )

    total_wait(group_in.at[:, 0:1], sum_recv.at[1])
    totals = group[0:1] + jnp.sum(group_in[:, 0:1], axis=0)
    totals_out[...] = jnp.broadcast_to(totals, (8, LANES)) / cell_count

    for copy in leaving:
        copy.wait()
    for copy in copies:
        copy.wait_send()
    total_wait(part_in.at[:, 0:1], sum_send.at[0])
    total_wait(group_in.at[:, 0:1], sum_send.at[1])


def margins(shape, stale_in, stale_hid, latent, weight_one, weight_two):
    tile_rows, tile_cols, channels = latent.shape
    n_row, n_col = shape
    strips = tile_rows // SH
    cell_count = float(tile_rows * tile_cols * n_row * n_col * (channels // GROUPS))
    hbm = pl.BlockSpec(memory_space=pltpu.HBM)
    vmem = pl.BlockSpec(memory_space=pltpu.VMEM)
    return pl.pallas_call(
        functools.partial(margins_kernel, cell_count, shape),
        out_shape=(
            jax.ShapeDtypeStruct((8, LANES), F32),
            jax.ShapeDtypeStruct((2, 2, strips, tile_cols, channels), BF16),
            jax.ShapeDtypeStruct((2, 2, tile_rows + 16, channels), F32),
            jax.ShapeDtypeStruct((tile_rows, tile_cols, channels), BF16),
            jax.ShapeDtypeStruct((4 * MAIN, 4 * MAIN), BF16),
            jax.ShapeDtypeStruct((4 * MAIN, 4 * MAIN), BF16),
        ),
        in_specs=[hbm] * 5,
        out_specs=(vmem,) * 4 + (hbm,) * 2,
        scratch_shapes=[
            pltpu.VMEM((2, tile_rows, tile_cols, channels), BF16),
            pltpu.VMEM((2, 4 * MAIN, 4 * MAIN), BF16),
            pltpu.VMEM((2,) + weight_one.shape, BF16),
            pltpu.VMEM((2, 2, tile_rows, channels), BF16),
            pltpu.VMEM((2, 2, tile_cols, channels), BF16),
            pltpu.VMEM((2, 2, tile_rows, channels), BF16),
            pltpu.VMEM((4, 2, 16, channels), BF16),
            pltpu.VMEM((8, LANES), F32),
            pltpu.VMEM((n_col // 2 - 1, 8, LANES), F32),
            pltpu.VMEM((8, LANES), F32),
            pltpu.VMEM((2 * n_row - 1, 8, LANES), F32),
            pltpu.SemaphoreType.DMA((2, 2)),
            pltpu.SemaphoreType.DMA((3,)),
            pltpu.SemaphoreType.DMA((2,)),
            pltpu.SemaphoreType.DMA((8,)),
            pltpu.SemaphoreType.DMA((8,)),
            pltpu.SemaphoreType.DMA((2,)),
            pltpu.SemaphoreType.DMA((2,)),
        ],
        compiler_params=pltpu.CompilerParams(
            collective_id=0, has_side_effects=True, vmem_limit_bytes=50 * 2**20
        ),
        name="margins",
    )(stale_in, stale_hid, latent, weight_one, weight_two)


def factors(totals, gains):
    channels = gains[0].shape[0]
    size = channels // GROUPS
    squares = pltpu.roll(totals, LANES - GROUPS, 1)
    lane_part = lax.div(lax.broadcasted_iota(jnp.int32, (8, LANES), 1), GROUPS)
    means = lax.rem(lane_part, 2) == 0
    spread = lax.rsqrt(jnp.where(means, squares - totals * totals, 1.0) + EPSILON)
    groups = lax.broadcasted_iota(jnp.int32, (LANES, channels), 0)
    members = lax.broadcasted_iota(jnp.int32, (LANES, channels), 1)
    parts = []
    for value in (totals[0:1], spread[0:1]):
        for _ in range(3):
            parts.append(value.astype(BF16).astype(F32))
            value = value - parts[-1]
    packed = jnp.concatenate(parts + [jnp.zeros((2, LANES), F32)], axis=0).astype(BF16)
    made = []
    for index, gain in enumerate(gains):
        own = (groups - 2 * GROUPS * index) * size
        valid = jnp.logical_and(groups >= 2 * GROUPS * index, groups < 2 * GROUPS * index + GROUPS)
        spill = one_hot(
            jnp.logical_and(valid, jnp.logical_and(members >= own, members < own + size)), BF16
        )
        spilt = jnp.dot(packed, spill, preferred_element_type=F32)
        center = spilt[0:1] + spilt[1:2] + spilt[2:3]
        scale = spilt[3:4] + spilt[4:5] + spilt[5:6]
        made.append((center, scale * gain[...].reshape(1, channels) * 0.5))
    return made


def strips_kernel(
    shape,
    refresh,
    totals,
    gain_one,
    gain_two,
    rows,
    cols,
    shift,
    tile,
    far_first,
    far_second,
    far_hidden,
    block_out,
    hidden_out,
    first_weights,
    second_weights,
    stale_hid,
    order,
    edges,
    sides,
    hidden,
    finished,
    load_sem,
    store_sem,
):
    tile_rows, tile_cols, channels = tile.shape
    strips = tile_rows // SH
    cells = SH * tile_cols
    packs = cells // 8
    apart = tile_cols // 8
    loads = [
        pltpu.make_async_copy(far_first, first_weights, load_sem.at[0]),
        pltpu.make_async_copy(far_second, second_weights, load_sem.at[1]),
        pltpu.make_async_copy(far_hidden, stale_hid, load_sem.at[2]),
    ]
    for copy in loads:
        copy.start()
    weights = (first_weights, second_weights)
    live_total = sum(refresh[0, strip] for strip in range(strips))
    pairs = lax.div(live_total + 1, 2)
    before = jnp.int32(0)
    for strip in range(strips):
        flag = refresh[0, strip]
        order[jnp.where(flag > 0, before, live_total + strip - before)] = jnp.int32(strip)
        before += flag
    n_row, n_col = shape
    row, col = lax.axis_index("row"), lax.axis_index("col")
    outside_rows = (row == 0, row == n_row - 1)
    outside_cols = (col == 0, col == n_col - 1)
    stats = factors(totals[...], (gain_one, gain_two))
    lines = lax.broadcasted_iota(jnp.int32, (cols.shape[2], 1), 0)
    beyond = jnp.logical_or(
        jnp.logical_and(lines == 0, outside_rows[0]),
        jnp.logical_and(lines == tile_rows + 1, outside_rows[1]),
    )
    for index in range(2):
        for side in range(2):
            value = act(cols[index, side], *stats[index])
            outside = jnp.logical_or(beyond, outside_cols[side])
            edges[index, side] = jnp.where(outside, 0.0, value)

    def margin_terms(index):
        for side in range(2):
            parts = [edges[index, side, a : a + tile_rows] for a in range(3)]
            lhs = side_by_side([part[:, :MAIN].astype(BF16) for part in parts], [tails(part) for part in parts])
            start = 2 * MAIN * side
            sides[index, side, :, :MAIN] = jnp.dot(
                lhs, weights[index][:, start : start + MAIN], preferred_element_type=F32
            )
            start = 3 * MAIN + LANES * side
            sides[index, side, :, MAIN:] = jnp.dot(
                lhs, weights[index][:, start : start + LANES], preferred_element_type=F32
            )
    sub = lax.broadcasted_iota(jnp.int32, (1, 8, 1), 1)

    def moved(index, side, strip, part, lanes):
        width = part.shape[-1]
        turned = pltpu.roll(part.reshape(packs, 8, width), 1 if side == 0 else 7, 1)
        pieces = []
        margin = sides[index, side, pl.ds(pl.multiple_of(strip * SH, SH), SH), lanes]
        for line in range(SH):
            edge = jnp.broadcast_to(margin[line : line + 1], (8, width))[None]
            first = line * apart
            if side == 0:
                pieces += [edge, turned[first : first + apart - 1]]
            else:
                pieces += [turned[first + 1 : first + apart], edge]
        carried = jnp.concatenate(pieces, axis=0)
        at = 0 if side == 0 else 7
        return jnp.where(sub == at, carried, turned).reshape(cells, width)

    def multiply(index, strip, inner):
        above, below = (
            act(rows[index, side, strip].astype(F32), *stats[index]) for side in range(2)
        )
        above = jnp.where(jnp.logical_and(strip == 0, outside_rows[0]), 0.0, above)
        below = jnp.where(jnp.logical_and(strip == strips - 1, outside_rows[1]), 0.0, below)
        values = jnp.concatenate([above[None], inner, below[None]], axis=0)
        main = values[..., :MAIN].astype(BF16)
        rest = tails(values)
        wide = side_by_side(
            [main[a : a + SH] for a in range(3)], [rest[a : a + SH] for a in range(3)]
        ).reshape(cells, 4 * MAIN)
        return [
            jnp.dot(
                wide,
                weights[index][:, part * MAIN : (part + 1) * MAIN],
                preferred_element_type=F32,
            )
            for part in range(4)
        ]

    def collect(index, strip, products):
        early, same, late, rest = products
        low, high = slice(0, MAIN), slice(MAIN, MAIN + LANES)
        main = moved(index, 0, strip, early, low) + same + moved(index, 1, strip, late, low)
        ends = (
            moved(index, 0, strip, rest[:, :LANES], high)
            + pltpu.roll(rest[:, :LANES], LANES // 2, 1)
            + moved(index, 1, strip, rest[:, LANES:], high)
        )
        return jnp.concatenate([main, ends[:, : channels - MAIN]], axis=1)

    loads[0].wait()
    margin_terms(0)
    for copy in loads[1:]:
        copy.wait()
    margin_terms(1)

    def one_pair(pair, carry):
        places = [order[2 * pair + local] for local in range(2)]
        spans = [pl.ds(strip * SH, SH) for strip in places]
        lives = [refresh[0, strip] > 0 for strip in places]
        fresh = [None, None]

        def begin(index, local):
            if index == 0:
                inner = act(tile[spans[local]].astype(F32), *stats[0])
            else:
                inner = act(fresh[local].astype(F32), *stats[1])
            return multiply(index, places[local], inner)

        def finish(index, local, products):
            span, live = spans[local], lives[local]
            summed = collect(index, places[local], products)
            if index == 0:
                value = (summed + shift[...].reshape(1, channels)).astype(BF16)
                fresh[local] = value.reshape(SH, tile_cols, channels)
                hidden[span] = jnp.where(live, fresh[local], stale_hid[span])
                made, out = hidden, hidden_out
            else:
                value = tile[span].astype(F32) + summed.reshape(SH, tile_cols, channels)
                finished[span] = jnp.where(live, value.astype(BF16), tile[span])
                made, out = finished, block_out
            pltpu.make_async_copy(made.at[span], out.at[span], store_sem.at[index]).start()

        waiting = None
        for index, local in ((0, 0), (0, 1), (1, 0), (1, 1)):
            products = begin(index, local)
            if waiting is not None:
                finish(*waiting)
            waiting = (index, local, products)
        finish(*waiting)
        return carry

    lax.fori_loop(0, pairs, one_pair, 0)
    for place in range(strips):

        @pl.when(place >= 2 * pairs)
        def _():
            span = pl.ds(order[place] * SH, SH)
            pltpu.make_async_copy(stale_hid.at[span], hidden_out.at[span], store_sem.at[0]).start()
            pltpu.make_async_copy(tile.at[span], block_out.at[span], store_sem.at[1]).start()

    total_wait(hidden, store_sem.at[0])
    total_wait(finished, store_sem.at[1])


def refreshed(
    shape,
    refresh,
    totals,
    gain_one,
    gain_two,
    rows,
    cols,
    shift,
    tile,
    first_weights,
    second_weights,
    stale_hid,
):
    tile_shape = tile.shape
    tile_rows, tile_cols, channels = tile_shape
    strip_total = tile_rows // SH
    anywhere = pl.BlockSpec(memory_space=pl.ANY)
    vmem = pl.BlockSpec(memory_space=pltpu.VMEM)
    out = jax.ShapeDtypeStruct(tile_shape, BF16)
    return pl.pallas_call(
        functools.partial(strips_kernel, shape),
        out_shape=(out, out),
        in_specs=[pl.BlockSpec(memory_space=pltpu.SMEM)] + [vmem] * 7 + [anywhere] * 3,
        out_specs=(anywhere, anywhere),
        scratch_shapes=[
            pltpu.VMEM((4 * MAIN, 4 * MAIN), BF16),
            pltpu.VMEM((4 * MAIN, 4 * MAIN), BF16),
            pltpu.VMEM(tile_shape, BF16),
            pltpu.SMEM((strip_total,), jnp.int32),
            pltpu.VMEM(cols.shape, F32),
            pltpu.VMEM((2, 2, tile_rows, MAIN + LANES), F32),
            pltpu.VMEM(tile_shape, BF16),
            pltpu.VMEM(tile_shape, BF16),
            pltpu.SemaphoreType.DMA((3,)),
            pltpu.SemaphoreType.DMA((2,)),
        ],
        compiler_params=pltpu.CompilerParams(vmem_limit_bytes=50 * 2**20),
        name="strips",
    )(
        refresh,
        totals,
        gain_one,
        gain_two,
        rows,
        cols,
        shift,
        tile,
        first_weights,
        second_weights,
        stale_hid,
    )


def per_device(
    shape,
    latent,
    stale_input,
    stale_hidden,
    refresh,
    gain_one,
    weight_one,
    time_shift,
    gain_two,
    weight_two,
):
    totals, rows, cols, tile, first_weights, second_weights = margins(
        shape, stale_input, stale_hidden, latent, weight_one, weight_two
    )
    return refreshed(
        shape,
        refresh.T,
        totals,
        gain_one,
        gain_two,
        rows,
        cols,
        time_shift,
        tile,
        first_weights,
        second_weights,
        stale_hidden,
    )


def solution(mesh):
    placed = (
        P("row", "col", None),
        P("row", "col", None),
        P("row", "col", None),
        P("row", "col"),
        P(),
        P(),
        P(),
        P(),
        P(),
    )
    return jax.shard_map(
        functools.partial(per_device, (mesh.shape["row"], mesh.shape["col"])),
        mesh=mesh,
        in_specs=placed,
        out_specs=(P("row", "col", None), P("row", "col", None)),
        check_vma=False,
    )
```

```python
import functools

import jax
import jax.numpy as jnp
from jax import lax
from jax.experimental import pallas as pl
from jax.experimental.pallas import tpu as pltpu
from jax.sharding import PartitionSpec as P

GROUPS = 32
SH = 8
EPSILON = 1e-05
LANES = 128
EXACT = lax.Precision.HIGHEST
F32 = jnp.float32
BF16 = jnp.bfloat16
MAIN = 256


def act(values, center, half_scale):
    half = (values - center) * half_scale
    return half * jnp.tanh(half) + half


def one_hot(condition, kind=F32):
    return jnp.where(condition, 1.0, 0.0).astype(kind)


def total_wait(buffer, semaphore):
    pltpu.make_async_copy(buffer, buffer, semaphore).wait()


def tails(values):
    rest = values[..., MAIN:]
    blank = jnp.zeros(rest.shape[:-1] + (LANES - rest.shape[-1],), rest.dtype)
    return jnp.concatenate([rest, blank], axis=-1)


def side_by_side(main, rest):
    turned = pltpu.roll(rest[1], LANES // 2, rest[1].ndim - 1)
    pairs = (rest[0] + turned).astype(BF16)
    return jnp.concatenate([*main, pairs, rest[2].astype(BF16)], axis=-1)


def margins_kernel(
    cell_count,
    shape,
    stale_in,
    stale_hid,
    latent,
    weight_one,
    weight_two,
    totals_out,
    rows_out,
    cols_out,
    tile_out,
    first_weights,
    second_weights,
    tiles,
    laid_out,
    raw,
    cols,
    rows_in,
    cols_in,
    corners_in,
    part,
    part_in,
    group,
    group_in,
    load_sem,
    late_sem,
    leave_sem,
    side_send,
    side_recv,
    sum_send,
    sum_recv,
):
    n_row, n_col = shape
    row, col = lax.axis_index("row"), lax.axis_index("col")
    tile_rows, tile_cols, channels = tiles.shape[1:]
    strips = tile_rows // SH
    up, down = lax.rem(row + n_row - 1, n_row), lax.rem(row + 1, n_row)
    left, right = lax.rem(col + n_col - 1, n_col), lax.rem(col + 1, n_col)
    core, x_high, z = lax.rem(col, 2), lax.rem(lax.div(col, 2), 2), lax.div(col, 4)
    y, x = lax.rem(row, 4), x_high * 2 + lax.div(row, 4)
    deep = n_col // 4
    first_peers, second_peers = 2 * deep - 1, 2 * n_row - 1

    def first_peer(step):
        place = lax.rem(z * 2 + core + lax.rem(step + deep - 1, first_peers) + 1, 2 * deep)
        return row, lax.div(place, 2) * 4 + x_high * 2 + lax.rem(place, 2)

    def second_peer(step):
        offset = lax.rem(step + 9, second_peers) + 1
        there_x, there_y = lax.rem(x + lax.div(offset, 4), 4), lax.rem(y + lax.rem(offset, 4), 4)
        there_row = lax.rem(there_x, 2) * 4 + there_y
        return there_row, z * 4 + lax.div(there_x, 2) * 2 + core

    def signal(device):
        pl.semaphore_signal(
            barrier, inc=1, device_id=device, device_id_type=pl.DeviceIdType.MESH
        )

    loads = []
    half = tile_rows // 2
    for index, source in enumerate((stale_in, stale_hid)):
        for piece in range(2):
            span = pl.ds(piece * half, half)
            copy = pltpu.make_async_copy(
                source.at[span], tiles.at[index, span], load_sem.at[index, piece]
            )
            copy.start()
            loads.append(copy)

    late = [
        pltpu.make_async_copy(weight_one, raw.at[0], late_sem.at[0]),
        pltpu.make_async_copy(weight_two, raw.at[1], late_sem.at[1]),
        pltpu.make_async_copy(latent, tile_out, late_sem.at[2]),
    ]
    for copy in late:
        copy.start()

    barrier = pltpu.get_barrier_semaphore()

    @pl.loop(0, first_peers)
    def _(step):
        signal(first_peer(step))
        signal(second_peer(step))

    for place in (up, row, down):
        for device in ((place, left), (place, right)):
            signal(device)
    signal((up, col))
    signal((down, col))

    lines = lax.broadcasted_iota(jnp.int32, (channels, LANES), 0)
    lanes = lax.rem(lax.broadcasted_iota(jnp.int32, (channels, LANES), 1), GROUPS)
    size = channels // GROUPS
    gather = one_hot(jnp.logical_and(lines >= lanes * size, lines < lanes * size + size))
    sums = []
    for index in range(2):
        zero = jnp.zeros((tile_cols, channels), F32)
        carry = (zero, zero)
        for piece in range(2):
            loads[2 * index + piece].wait()

            def add(line, carry):
                values = tiles[index, line].astype(F32)
                return carry[0] + values, carry[1] + values * values

            carry = lax.fori_loop(piece * half, (piece + 1) * half, add, carry, unroll=4)
        sums += [jnp.sum(carry[0], axis=0, keepdims=True), jnp.sum(carry[1], axis=0, keepdims=True)]
    stacked = jnp.concatenate(sums + [jnp.zeros((4, channels), F32)], axis=0)
    grouped = jnp.dot(stacked, gather, precision=EXACT, preferred_element_type=F32)
    lane_part = lax.div(lax.broadcasted_iota(jnp.int32, (8, LANES), 1), GROUPS)
    kept = jnp.where(lane_part == lax.broadcasted_iota(jnp.int32, (8, LANES), 0), grouped, 0.0)
    part[...] = jnp.broadcast_to(jnp.sum(kept, axis=0, keepdims=True), (8, LANES))

    pl.semaphore_wait(barrier, first_peers + second_peers + 8)

    def send_sums(source, target, peer, count, phase):
        @pl.loop(0, count)
        def _(step):
            pltpu.make_async_remote_copy(
                src_ref=source.at[0:1],
                dst_ref=target.at[step, 0:1],
                send_sem=sum_send.at[phase],
                recv_sem=sum_recv.at[phase],
                device_id=peer(step),
                device_id_type=pl.DeviceIdType.MESH,
            ).start()

    send_sums(part, part_in, first_peer, first_peers, 0)

    block = 16
    picks = lax.broadcasted_iota(jnp.int32, (2 * block, block * tile_cols), 0)
    cells = lax.broadcasted_iota(jnp.int32, (2 * block, block * tile_cols), 1)
    wanted = jnp.where(picks < block, picks * tile_cols, (picks - block) * tile_cols + tile_cols - 1)
    select = one_hot(cells == wanted, BF16)
    for index in range(2):
        for piece in range(tile_rows // block):
            span = pl.ds(piece * block, block)
            flat = tiles[index, span].reshape(block * tile_cols, channels)
            picked = jnp.dot(select, flat, preferred_element_type=F32).astype(BF16)
            cols[0, index, span] = picked[:block]
            cols[1, index, span] = picked[block:]

    head, tail = pl.ds(0, block), pl.ds(tile_rows - block, block)
    every = slice(None)
    moves = (
        (tiles.at[:, 0], rows_in.at[1], (up, col)),
        (tiles.at[:, tile_rows - 1], rows_in.at[0], (down, col)),
        (cols.at[0], cols_in.at[1], (row, left)),
        (cols.at[1], cols_in.at[0], (row, right)),
        (cols.at[0, every, head], corners_in.at[3], (up, left)),
        (cols.at[1, every, head], corners_in.at[2], (up, right)),
        (cols.at[0, every, tail], corners_in.at[1], (down, left)),
        (cols.at[1, every, tail], corners_in.at[0], (down, right)),
    )
    copies = []
    for index, (source, target, device) in enumerate(moves):
        copy = pltpu.make_async_remote_copy(
            src_ref=source,
            dst_ref=target,
            send_sem=side_send.at[index],
            recv_sem=side_recv.at[index],
            device_id=device,
            device_id_type=pl.DeviceIdType.MESH,
        )
        copy.start()
        copies.append(copy)

    leaving = []
    for index in range(2):
        late[index].wait()
        target = laid_out.at[index]
        for down_tap in range(3):
            taps = [raw[index, 3 * down_tap + across] for across in range(3)]
            rest = [tap[:, MAIN:] for tap in taps]
            blank = jnp.zeros_like(rest[0])
            ends = jnp.concatenate(rest + [blank], axis=1)
            pieces = [tap[:, :MAIN] for tap in taps] + [ends]
            for place, piece in enumerate(pieces):
                lanes = pl.ds(place * MAIN, MAIN)
                target[pl.ds(down_tap * MAIN, MAIN), lanes] = piece[:MAIN]
                spot = pl.ds(3 * MAIN + down_tap * (channels - MAIN), channels - MAIN)
                target[spot, lanes] = piece[MAIN:]
        spot = pl.ds(3 * channels, 4 * MAIN - 3 * channels)
        target[spot] = jnp.zeros((4 * MAIN - 3 * channels, 4 * MAIN), BF16)
        out = (first_weights, second_weights)[index]
        copy = pltpu.make_async_copy(target, out, leave_sem.at[index])
        copy.start()
        leaving.append(copy)
    late[2].wait()

    total_wait(part_in.at[:, 0:1], sum_recv.at[0])
    group[0:1] = part[0:1] + jnp.sum(part_in[:, 0:1], axis=0)
    send_sums(group, group_in, second_peer, second_peers, 1)
    def inner(strip, carry):
        for index in range(2):
            rows_out[index, 0, strip] = tiles[index, strip * SH - 1]
            rows_out[index, 1, strip - 1] = tiles[index, strip * SH]
        return carry

    lax.fori_loop(1, strips, inner, 0)
    for copy in copies:
        copy.wait_recv()
    for index in range(2):
        for side in range(2):
            rows_out[index, side, side * (strips - 1)] = rows_in[side, index]
            cols_out[index, side, 1 : tile_rows + 1] = cols_in[side, index].astype(F32)
            above, below = corners_in[side, index], corners_in[2 + side, index]
            cols_out[index, side, 0:1] = above.astype(F32)[block - 1 : block]
            cols_out[index, side, tile_rows + 1 :] = jnp.broadcast_to(
                below.astype(F32)[0:1], (15, channels)
            )

    total_wait(group_in.at[:, 0:1], sum_recv.at[1])
    totals = group[0:1] + jnp.sum(group_in[:, 0:1], axis=0)
    totals_out[...] = jnp.broadcast_to(totals, (8, LANES)) / cell_count

    for copy in leaving:
        copy.wait()
    for copy in copies:
        copy.wait_send()
    total_wait(part_in.at[:, 0:1], sum_send.at[0])
    total_wait(group_in.at[:, 0:1], sum_send.at[1])


def margins(shape, stale_in, stale_hid, latent, weight_one, weight_two):
    tile_rows, tile_cols, channels = latent.shape
    n_row, n_col = shape
    strips = tile_rows // SH
    cell_count = float(tile_rows * tile_cols * n_row * n_col * (channels // GROUPS))
    hbm = pl.BlockSpec(memory_space=pltpu.HBM)
    vmem = pl.BlockSpec(memory_space=pltpu.VMEM)
    return pl.pallas_call(
        functools.partial(margins_kernel, cell_count, shape),
        out_shape=(
            jax.ShapeDtypeStruct((8, LANES), F32),
            jax.ShapeDtypeStruct((2, 2, strips, tile_cols, channels), BF16),
            jax.ShapeDtypeStruct((2, 2, tile_rows + 16, channels), F32),
            jax.ShapeDtypeStruct((tile_rows, tile_cols, channels), BF16),
            jax.ShapeDtypeStruct((4 * MAIN, 4 * MAIN), BF16),
            jax.ShapeDtypeStruct((4 * MAIN, 4 * MAIN), BF16),
        ),
        in_specs=[hbm] * 5,
        out_specs=(vmem,) * 4 + (hbm,) * 2,
        scratch_shapes=[
            pltpu.VMEM((2, tile_rows, tile_cols, channels), BF16),
            pltpu.VMEM((2, 4 * MAIN, 4 * MAIN), BF16),
            pltpu.VMEM((2,) + weight_one.shape, BF16),
            pltpu.VMEM((2, 2, tile_rows, channels), BF16),
            pltpu.VMEM((2, 2, tile_cols, channels), BF16),
            pltpu.VMEM((2, 2, tile_rows, channels), BF16),
            pltpu.VMEM((4, 2, 16, channels), BF16),
            pltpu.VMEM((8, LANES), F32),
            pltpu.VMEM((n_col // 2 - 1, 8, LANES), F32),
            pltpu.VMEM((8, LANES), F32),
            pltpu.VMEM((2 * n_row - 1, 8, LANES), F32),
            pltpu.SemaphoreType.DMA((2, 2)),
            pltpu.SemaphoreType.DMA((3,)),
            pltpu.SemaphoreType.DMA((2,)),
            pltpu.SemaphoreType.DMA((8,)),
            pltpu.SemaphoreType.DMA((8,)),
            pltpu.SemaphoreType.DMA((2,)),
            pltpu.SemaphoreType.DMA((2,)),
        ],
        compiler_params=pltpu.CompilerParams(
            collective_id=0, has_side_effects=True, vmem_limit_bytes=50 * 2**20
        ),
        name="margins",
    )(stale_in, stale_hid, latent, weight_one, weight_two)


def factors(totals, gains):
    channels = gains[0].shape[0]
    size = channels // GROUPS
    squares = pltpu.roll(totals, LANES - GROUPS, 1)
    lane_part = lax.div(lax.broadcasted_iota(jnp.int32, (8, LANES), 1), GROUPS)
    means = lax.rem(lane_part, 2) == 0
    spread = lax.rsqrt(jnp.where(means, squares - totals * totals, 1.0) + EPSILON)
    groups = lax.broadcasted_iota(jnp.int32, (LANES, channels), 0)
    members = lax.broadcasted_iota(jnp.int32, (LANES, channels), 1)
    parts = []
    for value in (totals[0:1], spread[0:1]):
        for _ in range(3):
            parts.append(value.astype(BF16).astype(F32))
            value = value - parts[-1]
    packed = jnp.concatenate(parts + [jnp.zeros((2, LANES), F32)], axis=0).astype(BF16)
    made = []
    for index, gain in enumerate(gains):
        own = (groups - 2 * GROUPS * index) * size
        valid = jnp.logical_and(groups >= 2 * GROUPS * index, groups < 2 * GROUPS * index + GROUPS)
        spill = one_hot(
            jnp.logical_and(valid, jnp.logical_and(members >= own, members < own + size)), BF16
        )
        spilt = jnp.dot(packed, spill, preferred_element_type=F32)
        center = spilt[0:1] + spilt[1:2] + spilt[2:3]
        scale = spilt[3:4] + spilt[4:5] + spilt[5:6]
        made.append((center, scale * gain[...].reshape(1, channels) * 0.5))
    return made


def strips_kernel(
    shape,
    refresh,
    totals,
    gain_one,
    gain_two,
    rows,
    cols,
    shift,
    tile,
    far_first,
    far_second,
    far_hidden,
    block_out,
    hidden_out,
    first_weights,
    second_weights,
    stale_hid,
    order,
    edges,
    sides,
    hidden,
    finished,
    load_sem,
    store_sem,
):
    tile_rows, tile_cols, channels = tile.shape
    strips = tile_rows // SH
    cells = SH * tile_cols
    packs = cells // 8
    apart = tile_cols // 8
    loads = [
        pltpu.make_async_copy(far_first, first_weights, load_sem.at[0]),
        pltpu.make_async_copy(far_second, second_weights, load_sem.at[1]),
        pltpu.make_async_copy(far_hidden, stale_hid, load_sem.at[2]),
    ]
    for copy in loads:
        copy.start()
    weights = (first_weights, second_weights)
    live_total = sum(refresh[0, strip] for strip in range(strips))
    pairs = jnp.maximum(lax.div(live_total + 1, 2), 1)
    before = jnp.int32(0)
    for strip in range(strips):
        flag = refresh[0, strip]
        order[jnp.where(flag > 0, before, live_total + strip - before)] = jnp.int32(strip)
        before += flag
    n_row, n_col = shape
    row, col = lax.axis_index("row"), lax.axis_index("col")
    outside_rows = (row == 0, row == n_row - 1)
    outside_cols = (col == 0, col == n_col - 1)
    stats = factors(totals[...], (gain_one, gain_two))
    lines = lax.broadcasted_iota(jnp.int32, (cols.shape[2], 1), 0)
    beyond = jnp.logical_or(
        jnp.logical_and(lines == 0, outside_rows[0]),
        jnp.logical_and(lines == tile_rows + 1, outside_rows[1]),
    )
    for index in range(2):
        for side in range(2):
            value = act(cols[index, side], *stats[index])
            outside = jnp.logical_or(beyond, outside_cols[side])
            edges[index, side] = jnp.where(outside, 0.0, value)

    def margin_terms(index):
        for side in range(2):
            parts = [edges[index, side, a : a + tile_rows] for a in range(3)]
            lhs = side_by_side([part[:, :MAIN].astype(BF16) for part in parts], [tails(part) for part in parts])
            start = 2 * MAIN * side
            sides[index, side, :, :MAIN] = jnp.dot(
                lhs, weights[index][:, start : start + MAIN], preferred_element_type=F32
            )
            start = 3 * MAIN + LANES * side
            sides[index, side, :, MAIN:] = jnp.dot(
                lhs, weights[index][:, start : start + LANES], preferred_element_type=F32
            )
    sub = lax.broadcasted_iota(jnp.int32, (1, 8, 1), 1)

    def moved(index, side, strip, part, lanes):
        width = part.shape[-1]
        turned = pltpu.roll(part.reshape(packs, 8, width), 1 if side == 0 else 7, 1)
        pieces = []
        margin = sides[index, side, pl.ds(pl.multiple_of(strip * SH, SH), SH), lanes]
        for line in range(SH):
            edge = jnp.broadcast_to(margin[line : line + 1], (8, width))[None]
            first = line * apart
            if side == 0:
                pieces += [edge, turned[first : first + apart - 1]]
            else:
                pieces += [turned[first + 1 : first + apart], edge]
        carried = jnp.concatenate(pieces, axis=0)
        at = 0 if side == 0 else 7
        return jnp.where(sub == at, carried, turned).reshape(cells, width)

    def windows(index, strip, inner):
        above, below = (
            act(rows[index, side, strip].astype(F32), *stats[index]) for side in range(2)
        )
        above = jnp.where(jnp.logical_and(strip == 0, outside_rows[0]), 0.0, above)
        below = jnp.where(jnp.logical_and(strip == strips - 1, outside_rows[1]), 0.0, below)
        values = jnp.concatenate([above[None], inner, below[None]], axis=0)
        main = values[..., :MAIN].astype(BF16)
        rest = tails(values)
        return side_by_side(
            [main[a : a + SH] for a in range(3)], [rest[a : a + SH] for a in range(3)]
        ).reshape(cells, 4 * MAIN)

    def multiply(index, wide):
        return [
            jnp.dot(
                wide,
                weights[index][:, part * MAIN : (part + 1) * MAIN],
                preferred_element_type=F32,
            )
            for part in range(4)
        ]

    def collect(index, strip, products):
        early, same, late, rest = products
        low, high = slice(0, MAIN), slice(MAIN, MAIN + LANES)
        main = moved(index, 0, strip, early, low) + same + moved(index, 1, strip, late, low)
        ends = (
            moved(index, 0, strip, rest[:, :LANES], high)
            + pltpu.roll(rest[:, :LANES], LANES // 2, 1)
            + moved(index, 1, strip, rest[:, LANES:], high)
        )
        return jnp.concatenate([main, ends[:, : channels - MAIN]], axis=1)

    def one_pair(pair, carry, opening=False):
        places = [order[2 * pair + local] for local in range(2)]
        spans = [pl.ds(strip * SH, SH) for strip in places]
        lives = [refresh[0, strip] > 0 for strip in places]
        fresh = [None, None]

        def enter(index, local):
            if index == 0:
                inner = act(tile[spans[local]].astype(F32), *stats[0])
            else:
                inner = act(fresh[local].astype(F32), *stats[1])
            return windows(index, places[local], inner)

        def finish(index, local, products):
            span, live = spans[local], lives[local]
            summed = collect(index, places[local], products)
            if index == 0:
                value = (summed + shift[...].reshape(1, channels)).astype(BF16)
                fresh[local] = value.reshape(SH, tile_cols, channels)
                hidden[span] = jnp.where(live, fresh[local], stale_hid[span])
                made, out = hidden, hidden_out
            else:
                value = tile[span].astype(F32) + summed.reshape(SH, tile_cols, channels)
                finished[span] = jnp.where(live, value.astype(BF16), tile[span])
                made, out = finished, block_out
            pltpu.make_async_copy(made.at[span], out.at[span], store_sem.at[index]).start()

        wides = [enter(0, local) for local in range(2)]
        if opening:
            loads[0].wait()
        waiting = multiply(0, wides[0])
        products = multiply(0, wides[1])
        if opening:
            margin_terms(0)
            for copy in loads[1:]:
                copy.wait()
            margin_terms(1)
        finish(0, 0, waiting)
        waiting, products = products, multiply(1, enter(1, 0))
        finish(0, 1, waiting)
        waiting, products = products, multiply(1, enter(1, 1))
        finish(1, 0, waiting)
        finish(1, 1, products)
        return carry

    one_pair(0, 0, opening=True)
    for place in range(strips):

        @pl.when(place >= 2 * pairs)
        def _():
            span = pl.ds(order[place] * SH, SH)
            pltpu.make_async_copy(stale_hid.at[span], hidden_out.at[span], store_sem.at[0]).start()
            pltpu.make_async_copy(tile.at[span], block_out.at[span], store_sem.at[1]).start()

    lax.fori_loop(1, pairs, one_pair, 0)
    total_wait(hidden, store_sem.at[0])
    total_wait(finished, store_sem.at[1])


def refreshed(
    shape,
    refresh,
    totals,
    gain_one,
    gain_two,
    rows,
    cols,
    shift,
    tile,
    first_weights,
    second_weights,
    stale_hid,
):
    tile_shape = tile.shape
    tile_rows, tile_cols, channels = tile_shape
    strip_total = tile_rows // SH
    anywhere = pl.BlockSpec(memory_space=pl.ANY)
    vmem = pl.BlockSpec(memory_space=pltpu.VMEM)
    out = jax.ShapeDtypeStruct(tile_shape, BF16)
    return pl.pallas_call(
        functools.partial(strips_kernel, shape),
        out_shape=(out, out),
        in_specs=[pl.BlockSpec(memory_space=pltpu.SMEM)] + [vmem] * 7 + [anywhere] * 3,
        out_specs=(anywhere, anywhere),
        scratch_shapes=[
            pltpu.VMEM((4 * MAIN, 4 * MAIN), BF16),
            pltpu.VMEM((4 * MAIN, 4 * MAIN), BF16),
            pltpu.VMEM(tile_shape, BF16),
            pltpu.SMEM((strip_total,), jnp.int32),
            pltpu.VMEM(cols.shape, F32),
            pltpu.VMEM((2, 2, tile_rows, MAIN + LANES), F32),
            pltpu.VMEM(tile_shape, BF16),
            pltpu.VMEM(tile_shape, BF16),
            pltpu.SemaphoreType.DMA((3,)),
            pltpu.SemaphoreType.DMA((2,)),
        ],
        compiler_params=pltpu.CompilerParams(vmem_limit_bytes=50 * 2**20),
        name="strips",
    )(
        refresh,
        totals,
        gain_one,
        gain_two,
        rows,
        cols,
        shift,
        tile,
        first_weights,
        second_weights,
        stale_hid,
    )


def per_device(
    shape,
    latent,
    stale_input,
    stale_hidden,
    refresh,
    gain_one,
    weight_one,
    time_shift,
    gain_two,
    weight_two,
):
    totals, rows, cols, tile, first_weights, second_weights = margins(
        shape, stale_input, stale_hidden, latent, weight_one, weight_two
    )
    return refreshed(
        shape,
        refresh.T,
        totals,
        gain_one,
        gain_two,
        rows,
        cols,
        time_shift,
        tile,
        first_weights,
        second_weights,
        stale_hidden,
    )


def solution(mesh):
    placed = (
        P("row", "col", None),
        P("row", "col", None),
        P("row", "col", None),
        P("row", "col"),
        P(),
        P(),
        P(),
        P(),
        P(),
    )
    return jax.shard_map(
        functools.partial(per_device, (mesh.shape["row"], mesh.shape["col"])),
        mesh=mesh,
        in_specs=placed,
        out_specs=(P("row", "col", None), P("row", "col", None)),
        check_vma=False,
    )
```

```python
import functools

import jax
import jax.numpy as jnp
from jax import lax
from jax.experimental import pallas as pl
from jax.experimental.pallas import tpu as pltpu
from jax.sharding import PartitionSpec as P

GROUPS = 32
SH = 8
EPSILON = 1e-05
LANES = 128
EXACT = lax.Precision.HIGHEST
F32 = jnp.float32
BF16 = jnp.bfloat16
MAIN = 256
AHEAD = 4


def act(values, center, half_scale):
    half = (values - center) * half_scale
    return half * jnp.tanh(half) + half


def one_hot(condition, kind=F32):
    return jnp.where(condition, 1.0, 0.0).astype(kind)


def total_wait(buffer, semaphore):
    pltpu.make_async_copy(buffer, buffer, semaphore).wait()


def tails(values):
    rest = values[..., MAIN:]
    blank = jnp.zeros(rest.shape[:-1] + (LANES - rest.shape[-1],), rest.dtype)
    return jnp.concatenate([rest, blank], axis=-1)


def side_by_side(main, rest):
    turned = pltpu.roll(rest[1], LANES // 2, rest[1].ndim - 1)
    pairs = (rest[0] + turned).astype(BF16)
    return jnp.concatenate([*main, pairs, rest[2].astype(BF16)], axis=-1)


def margins_kernel(
    cell_count,
    shape,
    stale_in,
    stale_hid,
    latent,
    weight_one,
    weight_two,
    totals_out,
    rows_out,
    cols_out,
    tile_out,
    first_weights,
    second_weights,
    tiles,
    laid_out,
    raw,
    cols,
    rows_in,
    cols_in,
    corners_in,
    part,
    part_in,
    group,
    group_in,
    load_sem,
    late_sem,
    leave_sem,
    side_send,
    side_recv,
    sum_send,
    sum_recv,
):
    n_row, n_col = shape
    row, col = lax.axis_index("row"), lax.axis_index("col")
    tile_rows, tile_cols, channels = tiles.shape[1:]
    strips = tile_rows // SH
    up, down = lax.rem(row + n_row - 1, n_row), lax.rem(row + 1, n_row)
    left, right = lax.rem(col + n_col - 1, n_col), lax.rem(col + 1, n_col)
    core, x_high, z = lax.rem(col, 2), lax.rem(lax.div(col, 2), 2), lax.div(col, 4)
    y, x = lax.rem(row, 4), x_high * 2 + lax.div(row, 4)
    deep = n_col // 4
    first_peers, second_peers = 2 * deep - 1, 2 * n_row - 1

    def first_peer(step):
        place = lax.rem(z * 2 + core + lax.rem(step + deep - 1, first_peers) + 1, 2 * deep)
        return row, lax.div(place, 2) * 4 + x_high * 2 + lax.rem(place, 2)

    def second_peer(step):
        offset = lax.rem(step + 9, second_peers) + 1
        there_x, there_y = lax.rem(x + lax.div(offset, 4), 4), lax.rem(y + lax.rem(offset, 4), 4)
        there_row = lax.rem(there_x, 2) * 4 + there_y
        return there_row, z * 4 + lax.div(there_x, 2) * 2 + core

    def signal(device):
        pl.semaphore_signal(
            barrier, inc=1, device_id=device, device_id_type=pl.DeviceIdType.MESH
        )

    loads = []
    half = tile_rows // 2
    for index, source in enumerate((stale_in, stale_hid)):
        for piece in range(2):
            span = pl.ds(piece * half, half)
            copy = pltpu.make_async_copy(
                source.at[span], tiles.at[index, span], load_sem.at[index, piece]
            )
            copy.start()
            loads.append(copy)

    late = [
        pltpu.make_async_copy(weight_one, raw.at[0], late_sem.at[0]),
        pltpu.make_async_copy(weight_two, raw.at[1], late_sem.at[1]),
        pltpu.make_async_copy(latent, tile_out, late_sem.at[2]),
    ]
    for copy in late:
        copy.start()

    barrier = pltpu.get_barrier_semaphore()

    @pl.loop(0, first_peers)
    def _(step):
        signal(first_peer(step))
        signal(second_peer(step))

    for place in (up, row, down):
        for device in ((place, left), (place, right)):
            signal(device)
    signal((up, col))
    signal((down, col))

    lines = lax.broadcasted_iota(jnp.int32, (channels, LANES), 0)
    lanes = lax.rem(lax.broadcasted_iota(jnp.int32, (channels, LANES), 1), GROUPS)
    size = channels // GROUPS
    gather = one_hot(jnp.logical_and(lines >= lanes * size, lines < lanes * size + size))
    sums = []
    for index in range(2):
        zero = jnp.zeros((tile_cols, channels), F32)
        carry = (zero, zero)
        for piece in range(2):
            loads[2 * index + piece].wait()

            def add(line, carry):
                values = tiles[index, line].astype(F32)
                return carry[0] + values, carry[1] + values * values

            carry = lax.fori_loop(piece * half, (piece + 1) * half, add, carry, unroll=4)
        sums += [jnp.sum(carry[0], axis=0, keepdims=True), jnp.sum(carry[1], axis=0, keepdims=True)]
    stacked = jnp.concatenate(sums + [jnp.zeros((4, channels), F32)], axis=0)
    grouped = jnp.dot(stacked, gather, precision=EXACT, preferred_element_type=F32)
    lane_part = lax.div(lax.broadcasted_iota(jnp.int32, (8, LANES), 1), GROUPS)
    kept = jnp.where(lane_part == lax.broadcasted_iota(jnp.int32, (8, LANES), 0), grouped, 0.0)
    part[...] = jnp.broadcast_to(jnp.sum(kept, axis=0, keepdims=True), (8, LANES))

    pl.semaphore_wait(barrier, first_peers + second_peers + 8)

    def send_sums(source, target, peer, count, phase):
        @pl.loop(0, count)
        def _(step):
            pltpu.make_async_remote_copy(
                src_ref=source.at[0:1],
                dst_ref=target.at[step, 0:1],
                send_sem=sum_send.at[phase],
                recv_sem=sum_recv.at[phase],
                device_id=peer(step),
                device_id_type=pl.DeviceIdType.MESH,
            ).start()

    send_sums(part, part_in, first_peer, first_peers, 0)

    block = 16
    picks = lax.broadcasted_iota(jnp.int32, (2 * block, block * tile_cols), 0)
    cells = lax.broadcasted_iota(jnp.int32, (2 * block, block * tile_cols), 1)
    wanted = jnp.where(picks < block, picks * tile_cols, (picks - block) * tile_cols + tile_cols - 1)
    select = one_hot(cells == wanted, BF16)
    for index in range(2):
        for piece in range(tile_rows // block):
            span = pl.ds(piece * block, block)
            flat = tiles[index, span].reshape(block * tile_cols, channels)
            picked = jnp.dot(select, flat, preferred_element_type=F32).astype(BF16)
            cols[0, index, span] = picked[:block]
            cols[1, index, span] = picked[block:]

    head, tail = pl.ds(0, block), pl.ds(tile_rows - block, block)
    every = slice(None)
    moves = (
        (tiles.at[:, 0], rows_in.at[1], (up, col)),
        (tiles.at[:, tile_rows - 1], rows_in.at[0], (down, col)),
        (cols.at[0], cols_in.at[1], (row, left)),
        (cols.at[1], cols_in.at[0], (row, right)),
        (cols.at[0, every, head], corners_in.at[3], (up, left)),
        (cols.at[1, every, head], corners_in.at[2], (up, right)),
        (cols.at[0, every, tail], corners_in.at[1], (down, left)),
        (cols.at[1, every, tail], corners_in.at[0], (down, right)),
    )
    copies = []
    for index, (source, target, device) in enumerate(moves):
        copy = pltpu.make_async_remote_copy(
            src_ref=source,
            dst_ref=target,
            send_sem=side_send.at[index],
            recv_sem=side_recv.at[index],
            device_id=device,
            device_id_type=pl.DeviceIdType.MESH,
        )
        copy.start()
        copies.append(copy)

    leaving = []
    for index in range(2):
        late[index].wait()
        target = laid_out.at[index]
        for down_tap in range(3):
            taps = [raw[index, 3 * down_tap + across] for across in range(3)]
            rest = [tap[:, MAIN:] for tap in taps]
            blank = jnp.zeros_like(rest[0])
            ends = jnp.concatenate(rest + [blank], axis=1)
            pieces = [tap[:, :MAIN] for tap in taps] + [ends]
            for place, piece in enumerate(pieces):
                lanes = pl.ds(place * MAIN, MAIN)
                target[pl.ds(down_tap * MAIN, MAIN), lanes] = piece[:MAIN]
                spot = pl.ds(3 * MAIN + down_tap * (channels - MAIN), channels - MAIN)
                target[spot, lanes] = piece[MAIN:]
        spot = pl.ds(3 * channels, 4 * MAIN - 3 * channels)
        target[spot] = jnp.zeros((4 * MAIN - 3 * channels, 4 * MAIN), BF16)
        out = (first_weights, second_weights)[index]
        copy = pltpu.make_async_copy(target, out, leave_sem.at[index])
        copy.start()
        leaving.append(copy)
    late[2].wait()

    total_wait(part_in.at[:, 0:1], sum_recv.at[0])
    group[0:1] = part[0:1] + jnp.sum(part_in[:, 0:1], axis=0)
    send_sums(group, group_in, second_peer, second_peers, 1)
    def inner(strip, carry):
        for index in range(2):
            rows_out[index, 0, strip] = tiles[index, strip * SH - 1]
            rows_out[index, 1, strip - 1] = tiles[index, strip * SH]
        return carry

    lax.fori_loop(1, strips, inner, 0)
    for copy in copies:
        copy.wait_recv()
    for index in range(2):
        for side in range(2):
            rows_out[index, side, side * (strips - 1)] = rows_in[side, index]
            cols_out[index, side, 1 : tile_rows + 1] = cols_in[side, index].astype(F32)
            above, below = corners_in[side, index], corners_in[2 + side, index]
            cols_out[index, side, 0:1] = above.astype(F32)[block - 1 : block]
            cols_out[index, side, tile_rows + 1 :] = jnp.broadcast_to(
                below.astype(F32)[0:1], (15, channels)
            )

    total_wait(group_in.at[:, 0:1], sum_recv.at[1])
    totals = group[0:1] + jnp.sum(group_in[:, 0:1], axis=0)
    totals_out[...] = jnp.broadcast_to(totals, (8, LANES)) / cell_count

    for copy in leaving:
        copy.wait()
    for copy in copies:
        copy.wait_send()
    total_wait(part_in.at[:, 0:1], sum_send.at[0])
    total_wait(group_in.at[:, 0:1], sum_send.at[1])


def margins(shape, stale_in, stale_hid, latent, weight_one, weight_two):
    tile_rows, tile_cols, channels = latent.shape
    n_row, n_col = shape
    strips = tile_rows // SH
    cell_count = float(tile_rows * tile_cols * n_row * n_col * (channels // GROUPS))
    hbm = pl.BlockSpec(memory_space=pltpu.HBM)
    vmem = pl.BlockSpec(memory_space=pltpu.VMEM)
    return pl.pallas_call(
        functools.partial(margins_kernel, cell_count, shape),
        out_shape=(
            jax.ShapeDtypeStruct((8, LANES), F32),
            jax.ShapeDtypeStruct((2, 2, strips, tile_cols, channels), BF16),
            jax.ShapeDtypeStruct((2, 2, tile_rows + 16, channels), F32),
            jax.ShapeDtypeStruct((tile_rows, tile_cols, channels), BF16),
            jax.ShapeDtypeStruct((4 * MAIN, 4 * MAIN), BF16),
            jax.ShapeDtypeStruct((4 * MAIN, 4 * MAIN), BF16),
        ),
        in_specs=[hbm] * 5,
        out_specs=(vmem,) * 4 + (hbm,) * 2,
        scratch_shapes=[
            pltpu.VMEM((2, tile_rows, tile_cols, channels), BF16),
            pltpu.VMEM((2, 4 * MAIN, 4 * MAIN), BF16),
            pltpu.VMEM((2,) + weight_one.shape, BF16),
            pltpu.VMEM((2, 2, tile_rows, channels), BF16),
            pltpu.VMEM((2, 2, tile_cols, channels), BF16),
            pltpu.VMEM((2, 2, tile_rows, channels), BF16),
            pltpu.VMEM((4, 2, 16, channels), BF16),
            pltpu.VMEM((8, LANES), F32),
            pltpu.VMEM((n_col // 2 - 1, 8, LANES), F32),
            pltpu.VMEM((8, LANES), F32),
            pltpu.VMEM((2 * n_row - 1, 8, LANES), F32),
            pltpu.SemaphoreType.DMA((2, 2)),
            pltpu.SemaphoreType.DMA((3,)),
            pltpu.SemaphoreType.DMA((2,)),
            pltpu.SemaphoreType.DMA((8,)),
            pltpu.SemaphoreType.DMA((8,)),
            pltpu.SemaphoreType.DMA((2,)),
            pltpu.SemaphoreType.DMA((2,)),
        ],
        compiler_params=pltpu.CompilerParams(
            collective_id=0, has_side_effects=True, vmem_limit_bytes=50 * 2**20
        ),
        name="margins",
    )(stale_in, stale_hid, latent, weight_one, weight_two)


def factors(totals, gains):
    channels = gains[0].shape[0]
    size = channels // GROUPS
    squares = pltpu.roll(totals, LANES - GROUPS, 1)
    lane_part = lax.div(lax.broadcasted_iota(jnp.int32, (8, LANES), 1), GROUPS)
    means = lax.rem(lane_part, 2) == 0
    spread = lax.rsqrt(jnp.where(means, squares - totals * totals, 1.0) + EPSILON)
    groups = lax.broadcasted_iota(jnp.int32, (LANES, channels), 0)
    members = lax.broadcasted_iota(jnp.int32, (LANES, channels), 1)
    parts = []
    for value in (totals[0:1], spread[0:1]):
        for _ in range(3):
            parts.append(value.astype(BF16).astype(F32))
            value = value - parts[-1]
    packed = jnp.concatenate(parts + [jnp.zeros((2, LANES), F32)], axis=0).astype(BF16)
    made = []
    for index, gain in enumerate(gains):
        own = (groups - 2 * GROUPS * index) * size
        valid = jnp.logical_and(groups >= 2 * GROUPS * index, groups < 2 * GROUPS * index + GROUPS)
        spill = one_hot(
            jnp.logical_and(valid, jnp.logical_and(members >= own, members < own + size)), BF16
        )
        spilt = jnp.dot(packed, spill, preferred_element_type=F32)
        center = spilt[0:1] + spilt[1:2] + spilt[2:3]
        scale = spilt[3:4] + spilt[4:5] + spilt[5:6]
        made.append((center, scale * gain[...].reshape(1, channels) * 0.5))
    return made


def strips_kernel(
    shape,
    refresh,
    totals,
    gain_one,
    gain_two,
    rows,
    cols,
    shift,
    tile,
    far_first,
    far_second,
    far_hidden,
    block_out,
    hidden_out,
    first_weights,
    second_weights,
    stale_hid,
    order,
    edges,
    sides,
    hidden,
    finished,
    load_sem,
    store_sem,
):
    tile_rows, tile_cols, channels = tile.shape
    strips = tile_rows // SH
    cells = SH * tile_cols
    packs = cells // 8
    apart = tile_cols // 8
    loads = [
        pltpu.make_async_copy(far_first, first_weights, load_sem.at[0]),
        pltpu.make_async_copy(far_second, second_weights, load_sem.at[1]),
        pltpu.make_async_copy(far_hidden, stale_hid, load_sem.at[2]),
    ]
    for copy in loads:
        copy.start()
    weights = (first_weights, second_weights)
    live_total = sum(refresh[0, strip] for strip in range(strips))
    pairs = jnp.maximum(lax.div(live_total + 1, 2), 1)
    before = jnp.int32(0)
    for strip in range(strips):
        flag = refresh[0, strip]
        order[jnp.where(flag > 0, before, live_total + strip - before)] = jnp.int32(strip)
        before += flag
    n_row, n_col = shape
    row, col = lax.axis_index("row"), lax.axis_index("col")
    outside_rows = (row == 0, row == n_row - 1)
    outside_cols = (col == 0, col == n_col - 1)
    stats = factors(totals[...], (gain_one, gain_two))
    lines = lax.broadcasted_iota(jnp.int32, (cols.shape[2], 1), 0)
    beyond = jnp.logical_or(
        jnp.logical_and(lines == 0, outside_rows[0]),
        jnp.logical_and(lines == tile_rows + 1, outside_rows[1]),
    )
    for index in range(2):
        for side in range(2):
            value = act(cols[index, side], *stats[index])
            outside = jnp.logical_or(beyond, outside_cols[side])
            edges[index, side] = jnp.where(outside, 0.0, value)

    def margin_terms(index):
        for side in range(2):
            parts = [edges[index, side, a : a + tile_rows] for a in range(3)]
            lhs = side_by_side([part[:, :MAIN].astype(BF16) for part in parts], [tails(part) for part in parts])
            start = 2 * MAIN * side
            sides[index, side, :, :MAIN] = jnp.dot(
                lhs, weights[index][:, start : start + MAIN], preferred_element_type=F32
            )
            start = 3 * MAIN + LANES * side
            sides[index, side, :, MAIN:] = jnp.dot(
                lhs, weights[index][:, start : start + LANES], preferred_element_type=F32
            )
    sub = lax.broadcasted_iota(jnp.int32, (1, 8, 1), 1)

    def moved(index, side, strip, part, lanes):
        width = part.shape[-1]
        turned = pltpu.roll(part.reshape(packs, 8, width), 1 if side == 0 else 7, 1)
        pieces = []
        margin = sides[index, side, pl.ds(pl.multiple_of(strip * SH, SH), SH), lanes]
        for line in range(SH):
            edge = jnp.broadcast_to(margin[line : line + 1], (8, width))[None]
            first = line * apart
            if side == 0:
                pieces += [edge, turned[first : first + apart - 1]]
            else:
                pieces += [turned[first + 1 : first + apart], edge]
        carried = jnp.concatenate(pieces, axis=0)
        at = 0 if side == 0 else 7
        return jnp.where(sub == at, carried, turned).reshape(cells, width)

    def windows(index, strip, inner):
        above, below = (
            act(rows[index, side, strip].astype(F32), *stats[index]) for side in range(2)
        )
        above = jnp.where(jnp.logical_and(strip == 0, outside_rows[0]), 0.0, above)
        below = jnp.where(jnp.logical_and(strip == strips - 1, outside_rows[1]), 0.0, below)
        values = jnp.concatenate([above[None], inner, below[None]], axis=0)
        main = values[..., :MAIN].astype(BF16)
        rest = tails(values)
        return side_by_side(
            [main[a : a + SH] for a in range(3)], [rest[a : a + SH] for a in range(3)]
        ).reshape(cells, 4 * MAIN)

    def multiply(index, wide):
        return [
            jnp.dot(
                wide,
                weights[index][:, part * MAIN : (part + 1) * MAIN],
                preferred_element_type=F32,
            )
            for part in range(4)
        ]

    def collect(index, strip, products):
        early, same, late, rest = products
        low, high = slice(0, MAIN), slice(MAIN, MAIN + LANES)
        main = moved(index, 0, strip, early, low) + same + moved(index, 1, strip, late, low)
        ends = (
            moved(index, 0, strip, rest[:, :LANES], high)
            + pltpu.roll(rest[:, :LANES], LANES // 2, 1)
            + moved(index, 1, strip, rest[:, LANES:], high)
        )
        return jnp.concatenate([main, ends[:, : channels - MAIN]], axis=1)

    def straight(places, others):
        fresh = {}

        def span_of(place):
            return pl.ds(places[place] * SH, SH)

        def begin(index, place):
            if index == 0:
                inner = act(tile[span_of(place)].astype(F32), *stats[0])
            else:
                inner = act(fresh[place].astype(F32), *stats[1])
            return multiply(index, windows(index, places[place], inner))

        def finish(index, place, products):
            span, live = span_of(place), refresh[0, places[place]] > 0
            summed = collect(index, places[place], products)
            if index == 0:
                value = (summed + shift[...].reshape(1, channels)).astype(BF16)
                fresh[place] = value.reshape(SH, tile_cols, channels)
                hidden[span] = jnp.where(live, fresh[place], stale_hid[span])
                made, out = hidden, hidden_out
            else:
                value = tile[span].astype(F32) + summed.reshape(SH, tile_cols, channels)
                finished[span] = jnp.where(live, value.astype(BF16), tile[span])
                made, out = finished, block_out
            pltpu.make_async_copy(made.at[span], out.at[span], store_sem.at[index]).start()

        loads[0].wait()
        margin_terms(0)
        waiting, waited = [], False
        for start in range(0, len(places), AHEAD):
            for index in range(2):
                for place in range(start, min(start + AHEAD, len(places))):
                    waiting.append((index, place, begin(index, place)))
                    if len(waiting) < 2:
                        continue
                    if not waited:
                        for copy in loads[1:]:
                            copy.wait()
                        margin_terms(1)
                        for strip in others:
                            span = pl.ds(strip * SH, SH)
                            pltpu.make_async_copy(
                                stale_hid.at[span], hidden_out.at[span], store_sem.at[0]
                            ).start()
                            pltpu.make_async_copy(
                                tile.at[span], block_out.at[span], store_sem.at[1]
                            ).start()
                        waited = True
                    finish(*waiting.pop(0))
        finish(*waiting.pop(0))

    for count in range(1, strips // 2 + 1):

        @pl.when(pairs == count)
        def _():
            if 2 * count == strips:
                listed = list(range(strips))
            else:
                listed = [order[place] for place in range(strips)]
            straight(listed[: 2 * count], listed[2 * count :])

    total_wait(hidden, store_sem.at[0])
    total_wait(finished, store_sem.at[1])


def refreshed(
    shape,
    refresh,
    totals,
    gain_one,
    gain_two,
    rows,
    cols,
    shift,
    tile,
    first_weights,
    second_weights,
    stale_hid,
):
    tile_shape = tile.shape
    tile_rows, tile_cols, channels = tile_shape
    strip_total = tile_rows // SH
    anywhere = pl.BlockSpec(memory_space=pl.ANY)
    vmem = pl.BlockSpec(memory_space=pltpu.VMEM)
    out = jax.ShapeDtypeStruct(tile_shape, BF16)
    return pl.pallas_call(
        functools.partial(strips_kernel, shape),
        out_shape=(out, out),
        in_specs=[pl.BlockSpec(memory_space=pltpu.SMEM)] + [vmem] * 7 + [anywhere] * 3,
        out_specs=(anywhere, anywhere),
        scratch_shapes=[
            pltpu.VMEM((4 * MAIN, 4 * MAIN), BF16),
            pltpu.VMEM((4 * MAIN, 4 * MAIN), BF16),
            pltpu.VMEM(tile_shape, BF16),
            pltpu.SMEM((strip_total,), jnp.int32),
            pltpu.VMEM(cols.shape, F32),
            pltpu.VMEM((2, 2, tile_rows, MAIN + LANES), F32),
            pltpu.VMEM(tile_shape, BF16),
            pltpu.VMEM(tile_shape, BF16),
            pltpu.SemaphoreType.DMA((3,)),
            pltpu.SemaphoreType.DMA((2,)),
        ],
        compiler_params=pltpu.CompilerParams(vmem_limit_bytes=50 * 2**20),
        name="strips",
    )(
        refresh,
        totals,
        gain_one,
        gain_two,
        rows,
        cols,
        shift,
        tile,
        first_weights,
        second_weights,
        stale_hid,
    )


def per_device(
    shape,
    latent,
    stale_input,
    stale_hidden,
    refresh,
    gain_one,
    weight_one,
    time_shift,
    gain_two,
    weight_two,
):
    totals, rows, cols, tile, first_weights, second_weights = margins(
        shape, stale_input, stale_hidden, latent, weight_one, weight_two
    )
    return refreshed(
        shape,
        refresh.T,
        totals,
        gain_one,
        gain_two,
        rows,
        cols,
        time_shift,
        tile,
        first_weights,
        second_weights,
        stale_hidden,
    )


def solution(mesh):
    placed = (
        P("row", "col", None),
        P("row", "col", None),
        P("row", "col", None),
        P("row", "col"),
        P(),
        P(),
        P(),
        P(),
        P(),
    )
    return jax.shard_map(
        functools.partial(per_device, (mesh.shape["row"], mesh.shape["col"])),
        mesh=mesh,
        in_specs=placed,
        out_specs=(P("row", "col", None), P("row", "col", None)),
        check_vma=False,
    )
```

```python
import functools

import jax
import jax.numpy as jnp
from jax import lax
from jax.experimental import pallas as pl
from jax.experimental.pallas import tpu as pltpu
from jax.sharding import PartitionSpec as P

GROUPS = 32
SH = 8
EPSILON = 1e-05
LANES = 128
EXACT = lax.Precision.HIGHEST
F32 = jnp.float32
BF16 = jnp.bfloat16
MAIN = 256
AHEAD = 4


def act(values, center, half_scale):
    half = (values - center) * half_scale
    return half * jnp.tanh(half) + half


def one_hot(condition, kind=F32):
    return jnp.where(condition, 1.0, 0.0).astype(kind)


def total_wait(buffer, semaphore):
    pltpu.make_async_copy(buffer, buffer, semaphore).wait()


def tails(values):
    rest = values[..., MAIN:]
    blank = jnp.zeros(rest.shape[:-1] + (LANES - rest.shape[-1],), rest.dtype)
    return jnp.concatenate([rest, blank], axis=-1)


def side_by_side(main, rest):
    turned = pltpu.roll(rest[1], LANES // 2, rest[1].ndim - 1)
    pairs = (rest[0] + turned).astype(BF16)
    return jnp.concatenate([*main, pairs, rest[2].astype(BF16)], axis=-1)


def margins_kernel(
    cell_count,
    shape,
    stale_in,
    stale_hid,
    latent,
    weight_one,
    weight_two,
    totals_out,
    rows_out,
    cols_out,
    tile_out,
    first_weights,
    second_weights,
    tiles,
    laid_out,
    raw,
    cols,
    rows_in,
    cols_in,
    corners_in,
    part,
    part_in,
    group,
    group_in,
    load_sem,
    late_sem,
    leave_sem,
    side_send,
    side_recv,
    sum_send,
    sum_recv,
):
    n_row, n_col = shape
    row, col = lax.axis_index("row"), lax.axis_index("col")
    tile_rows, tile_cols, channels = tiles.shape[1:]
    strips = tile_rows // SH
    up, down = lax.rem(row + n_row - 1, n_row), lax.rem(row + 1, n_row)
    left, right = lax.rem(col + n_col - 1, n_col), lax.rem(col + 1, n_col)
    core, x_high, z = lax.rem(col, 2), lax.rem(lax.div(col, 2), 2), lax.div(col, 4)
    y, x = lax.rem(row, 4), x_high * 2 + lax.div(row, 4)
    deep = n_col // 4
    first_peers, second_peers = 2 * deep - 1, 2 * n_row - 1

    def first_peer(step):
        place = lax.rem(z * 2 + core + lax.rem(step + deep - 1, first_peers) + 1, 2 * deep)
        return row, lax.div(place, 2) * 4 + x_high * 2 + lax.rem(place, 2)

    def second_peer(step):
        offset = lax.rem(step + 9, second_peers) + 1
        there_x, there_y = lax.rem(x + lax.div(offset, 4), 4), lax.rem(y + lax.rem(offset, 4), 4)
        there_row = lax.rem(there_x, 2) * 4 + there_y
        return there_row, z * 4 + lax.div(there_x, 2) * 2 + core

    def signal(device):
        pl.semaphore_signal(
            barrier, inc=1, device_id=device, device_id_type=pl.DeviceIdType.MESH
        )

    barrier = pltpu.get_barrier_semaphore()

    @pl.loop(0, first_peers)
    def _(step):
        signal(first_peer(step))
        signal(second_peer(step))

    for place in (up, row, down):
        for device in ((place, left), (place, right)):
            signal(device)
    signal((up, col))
    signal((down, col))

    loads = []
    half = tile_rows // 2
    for index, source in enumerate((stale_in, stale_hid)):
        for piece in range(2):
            span = pl.ds(piece * half, half)
            copy = pltpu.make_async_copy(
                source.at[span], tiles.at[index, span], load_sem.at[index, piece]
            )
            copy.start()
            loads.append(copy)

    late = [
        pltpu.make_async_copy(weight_one, raw.at[0], late_sem.at[0]),
        pltpu.make_async_copy(weight_two, raw.at[1], late_sem.at[1]),
        pltpu.make_async_copy(latent, tile_out, late_sem.at[2]),
    ]
    for copy in late:
        copy.start()

    lines = lax.broadcasted_iota(jnp.int32, (channels, LANES), 0)
    lanes = lax.rem(lax.broadcasted_iota(jnp.int32, (channels, LANES), 1), GROUPS)
    size = channels // GROUPS
    gather = one_hot(jnp.logical_and(lines >= lanes * size, lines < lanes * size + size))
    sums = []
    for index in range(2):
        zero = jnp.zeros((tile_cols, channels), F32)
        carry = (zero, zero)
        for piece in range(2):
            loads[2 * index + piece].wait()

            def add(line, carry):
                values = tiles[index, line].astype(F32)
                return carry[0] + values, carry[1] + values * values

            carry = lax.fori_loop(piece * half, (piece + 1) * half, add, carry, unroll=4)
        sums += [jnp.sum(carry[0], axis=0, keepdims=True), jnp.sum(carry[1], axis=0, keepdims=True)]
    stacked = jnp.concatenate(sums + [jnp.zeros((4, channels), F32)], axis=0)
    grouped = jnp.dot(stacked, gather, precision=EXACT, preferred_element_type=F32)
    lane_part = lax.div(lax.broadcasted_iota(jnp.int32, (8, LANES), 1), GROUPS)
    kept = jnp.where(lane_part == lax.broadcasted_iota(jnp.int32, (8, LANES), 0), grouped, 0.0)
    part[...] = jnp.broadcast_to(jnp.sum(kept, axis=0, keepdims=True), (8, LANES))

    pl.semaphore_wait(barrier, first_peers + second_peers + 8)

    def send_sums(source, target, peer, count, phase):
        @pl.loop(0, count)
        def _(step):
            pltpu.make_async_remote_copy(
                src_ref=source.at[0:1],
                dst_ref=target.at[step, 0:1],
                send_sem=sum_send.at[phase],
                recv_sem=sum_recv.at[phase],
                device_id=peer(step),
                device_id_type=pl.DeviceIdType.MESH,
            ).start()

    send_sums(part, part_in, first_peer, first_peers, 0)

    block = 16
    picks = lax.broadcasted_iota(jnp.int32, (2 * block, block * tile_cols), 0)
    cells = lax.broadcasted_iota(jnp.int32, (2 * block, block * tile_cols), 1)
    wanted = jnp.where(picks < block, picks * tile_cols, (picks - block) * tile_cols + tile_cols - 1)
    select = one_hot(cells == wanted, BF16)
    for index in range(2):
        for piece in range(tile_rows // block):
            span = pl.ds(piece * block, block)
            flat = tiles[index, span].reshape(block * tile_cols, channels)
            picked = jnp.dot(select, flat, preferred_element_type=F32).astype(BF16)
            cols[0, index, span] = picked[:block]
            cols[1, index, span] = picked[block:]

    head, tail = pl.ds(0, block), pl.ds(tile_rows - block, block)
    every = slice(None)
    moves = (
        (tiles.at[:, 0], rows_in.at[1], (up, col)),
        (tiles.at[:, tile_rows - 1], rows_in.at[0], (down, col)),
        (cols.at[0], cols_in.at[1], (row, left)),
        (cols.at[1], cols_in.at[0], (row, right)),
        (cols.at[0, every, head], corners_in.at[3], (up, left)),
        (cols.at[1, every, head], corners_in.at[2], (up, right)),
        (cols.at[0, every, tail], corners_in.at[1], (down, left)),
        (cols.at[1, every, tail], corners_in.at[0], (down, right)),
    )
    copies = []
    for index, (source, target, device) in enumerate(moves):
        copy = pltpu.make_async_remote_copy(
            src_ref=source,
            dst_ref=target,
            send_sem=side_send.at[index],
            recv_sem=side_recv.at[index],
            device_id=device,
            device_id_type=pl.DeviceIdType.MESH,
        )
        copy.start()
        copies.append(copy)

    leaving = []
    for index in range(2):
        late[index].wait()
        target = laid_out.at[index]
        for down_tap in range(3):
            taps = [raw[index, 3 * down_tap + across] for across in range(3)]
            rest = [tap[:, MAIN:] for tap in taps]
            blank = jnp.zeros_like(rest[0])
            ends = jnp.concatenate(rest + [blank], axis=1)
            pieces = [tap[:, :MAIN] for tap in taps] + [ends]
            for place, piece in enumerate(pieces):
                lanes = pl.ds(place * MAIN, MAIN)
                target[pl.ds(down_tap * MAIN, MAIN), lanes] = piece[:MAIN]
                spot = pl.ds(3 * MAIN + down_tap * (channels - MAIN), channels - MAIN)
                target[spot, lanes] = piece[MAIN:]
        spot = pl.ds(3 * channels, 4 * MAIN - 3 * channels)
        target[spot] = jnp.zeros((4 * MAIN - 3 * channels, 4 * MAIN), BF16)
        out = (first_weights, second_weights)[index]
        copy = pltpu.make_async_copy(target, out, leave_sem.at[index])
        copy.start()
        leaving.append(copy)
    late[2].wait()

    total_wait(part_in.at[:, 0:1], sum_recv.at[0])
    group[0:1] = part[0:1] + jnp.sum(part_in[:, 0:1], axis=0)
    send_sums(group, group_in, second_peer, second_peers, 1)
    def inner(strip, carry):
        for index in range(2):
            rows_out[index, 0, strip] = tiles[index, strip * SH - 1]
            rows_out[index, 1, strip - 1] = tiles[index, strip * SH]
        return carry

    lax.fori_loop(1, strips, inner, 0)
    for copy in copies:
        copy.wait_recv()
    for index in range(2):
        for side in range(2):
            rows_out[index, side, side * (strips - 1)] = rows_in[side, index]
            cols_out[index, side, 1 : tile_rows + 1] = cols_in[side, index].astype(F32)
            above, below = corners_in[side, index], corners_in[2 + side, index]
            cols_out[index, side, 0:1] = above.astype(F32)[block - 1 : block]
            cols_out[index, side, tile_rows + 1 :] = jnp.broadcast_to(
                below.astype(F32)[0:1], (15, channels)
            )

    total_wait(group_in.at[:, 0:1], sum_recv.at[1])
    totals = group[0:1] + jnp.sum(group_in[:, 0:1], axis=0)
    totals_out[...] = jnp.broadcast_to(totals, (8, LANES)) / cell_count

    for copy in leaving:
        copy.wait()
    for copy in copies:
        copy.wait_send()
    total_wait(part_in.at[:, 0:1], sum_send.at[0])
    total_wait(group_in.at[:, 0:1], sum_send.at[1])


def margins(shape, stale_in, stale_hid, latent, weight_one, weight_two):
    tile_rows, tile_cols, channels = latent.shape
    n_row, n_col = shape
    strips = tile_rows // SH
    cell_count = float(tile_rows * tile_cols * n_row * n_col * (channels // GROUPS))
    hbm = pl.BlockSpec(memory_space=pltpu.HBM)
    vmem = pl.BlockSpec(memory_space=pltpu.VMEM)
    return pl.pallas_call(
        functools.partial(margins_kernel, cell_count, shape),
        out_shape=(
            jax.ShapeDtypeStruct((8, LANES), F32),
            jax.ShapeDtypeStruct((2, 2, strips, tile_cols, channels), BF16),
            jax.ShapeDtypeStruct((2, 2, tile_rows + 16, channels), F32),
            jax.ShapeDtypeStruct((tile_rows, tile_cols, channels), BF16),
            jax.ShapeDtypeStruct((4 * MAIN, 4 * MAIN), BF16),
            jax.ShapeDtypeStruct((4 * MAIN, 4 * MAIN), BF16),
        ),
        in_specs=[hbm] * 5,
        out_specs=(vmem,) * 4 + (hbm,) * 2,
        scratch_shapes=[
            pltpu.VMEM((2, tile_rows, tile_cols, channels), BF16),
            pltpu.VMEM((2, 4 * MAIN, 4 * MAIN), BF16),
            pltpu.VMEM((2,) + weight_one.shape, BF16),
            pltpu.VMEM((2, 2, tile_rows, channels), BF16),
            pltpu.VMEM((2, 2, tile_cols, channels), BF16),
            pltpu.VMEM((2, 2, tile_rows, channels), BF16),
            pltpu.VMEM((4, 2, 16, channels), BF16),
            pltpu.VMEM((8, LANES), F32),
            pltpu.VMEM((n_col // 2 - 1, 8, LANES), F32),
            pltpu.VMEM((8, LANES), F32),
            pltpu.VMEM((2 * n_row - 1, 8, LANES), F32),
            pltpu.SemaphoreType.DMA((2, 2)),
            pltpu.SemaphoreType.DMA((3,)),
            pltpu.SemaphoreType.DMA((2,)),
            pltpu.SemaphoreType.DMA((8,)),
            pltpu.SemaphoreType.DMA((8,)),
            pltpu.SemaphoreType.DMA((2,)),
            pltpu.SemaphoreType.DMA((2,)),
        ],
        compiler_params=pltpu.CompilerParams(
            collective_id=0, has_side_effects=True, vmem_limit_bytes=50 * 2**20
        ),
        name="margins",
    )(stale_in, stale_hid, latent, weight_one, weight_two)


def factors(totals, gains):
    channels = gains[0].shape[0]
    size = channels // GROUPS
    squares = pltpu.roll(totals, LANES - GROUPS, 1)
    lane_part = lax.div(lax.broadcasted_iota(jnp.int32, (8, LANES), 1), GROUPS)
    means = lax.rem(lane_part, 2) == 0
    spread = lax.rsqrt(jnp.where(means, squares - totals * totals, 1.0) + EPSILON)
    groups = lax.broadcasted_iota(jnp.int32, (LANES, channels), 0)
    members = lax.broadcasted_iota(jnp.int32, (LANES, channels), 1)
    parts = []
    for value in (totals[0:1], spread[0:1]):
        for _ in range(3):
            parts.append(value.astype(BF16).astype(F32))
            value = value - parts[-1]
    packed = jnp.concatenate(parts + [jnp.zeros((2, LANES), F32)], axis=0).astype(BF16)
    made = []
    for index, gain in enumerate(gains):
        own = (groups - 2 * GROUPS * index) * size
        valid = jnp.logical_and(groups >= 2 * GROUPS * index, groups < 2 * GROUPS * index + GROUPS)
        spill = one_hot(
            jnp.logical_and(valid, jnp.logical_and(members >= own, members < own + size)), BF16
        )
        spilt = jnp.dot(packed, spill, preferred_element_type=F32)
        center = spilt[0:1] + spilt[1:2] + spilt[2:3]
        scale = spilt[3:4] + spilt[4:5] + spilt[5:6]
        made.append((center, scale * gain[...].reshape(1, channels) * 0.5))
    return made


def strips_kernel(
    shape,
    refresh,
    totals,
    gain_one,
    gain_two,
    rows,
    cols,
    shift,
    tile,
    far_first,
    far_second,
    far_hidden,
    block_out,
    hidden_out,
    first_weights,
    second_weights,
    stale_hid,
    order,
    edges,
    sides,
    hidden,
    finished,
    load_sem,
    store_sem,
):
    tile_rows, tile_cols, channels = tile.shape
    strips = tile_rows // SH
    cells = SH * tile_cols
    packs = cells // 8
    apart = tile_cols // 8
    loads = [
        pltpu.make_async_copy(far_first, first_weights, load_sem.at[0]),
        pltpu.make_async_copy(far_second, second_weights, load_sem.at[1]),
        pltpu.make_async_copy(far_hidden, stale_hid, load_sem.at[2]),
    ]
    for copy in loads:
        copy.start()
    weights = (first_weights, second_weights)
    live_total = sum(refresh[0, strip] for strip in range(strips))
    pairs = jnp.maximum(lax.div(live_total + 1, 2), 1)
    before = jnp.int32(0)
    for strip in range(strips):
        flag = refresh[0, strip]
        order[jnp.where(flag > 0, before, live_total + strip - before)] = jnp.int32(strip)
        before += flag
    n_row, n_col = shape
    row, col = lax.axis_index("row"), lax.axis_index("col")
    outside_rows = (row == 0, row == n_row - 1)
    outside_cols = (col == 0, col == n_col - 1)
    stats = factors(totals[...], (gain_one, gain_two))
    lines = lax.broadcasted_iota(jnp.int32, (cols.shape[2], 1), 0)
    beyond = jnp.logical_or(
        jnp.logical_and(lines == 0, outside_rows[0]),
        jnp.logical_and(lines == tile_rows + 1, outside_rows[1]),
    )
    for index in range(2):
        for side in range(2):
            value = act(cols[index, side], *stats[index])
            outside = jnp.logical_or(beyond, outside_cols[side])
            edges[index, side] = jnp.where(outside, 0.0, value)

    def margin_terms(index):
        for side in range(2):
            parts = [edges[index, side, a : a + tile_rows] for a in range(3)]
            lhs = side_by_side([part[:, :MAIN].astype(BF16) for part in parts], [tails(part) for part in parts])
            start = 2 * MAIN * side
            sides[index, side, :, :MAIN] = jnp.dot(
                lhs, weights[index][:, start : start + MAIN], preferred_element_type=F32
            )
            start = 3 * MAIN + LANES * side
            sides[index, side, :, MAIN:] = jnp.dot(
                lhs, weights[index][:, start : start + LANES], preferred_element_type=F32
            )
    sub = lax.broadcasted_iota(jnp.int32, (1, 8, 1), 1)

    def moved(index, side, strip, part, lanes):
        width = part.shape[-1]
        turned = pltpu.roll(part.reshape(packs, 8, width), 1 if side == 0 else 7, 1)
        pieces = []
        margin = sides[index, side, pl.ds(pl.multiple_of(strip * SH, SH), SH), lanes]
        for line in range(SH):
            edge = jnp.broadcast_to(margin[line : line + 1], (8, width))[None]
            first = line * apart
            if side == 0:
                pieces += [edge, turned[first : first + apart - 1]]
            else:
                pieces += [turned[first + 1 : first + apart], edge]
        carried = jnp.concatenate(pieces, axis=0)
        at = 0 if side == 0 else 7
        return jnp.where(sub == at, carried, turned).reshape(cells, width)

    def windows(index, strip, inner):
        above, below = (
            act(rows[index, side, strip].astype(F32), *stats[index]) for side in range(2)
        )
        above = jnp.where(jnp.logical_and(strip == 0, outside_rows[0]), 0.0, above)
        below = jnp.where(jnp.logical_and(strip == strips - 1, outside_rows[1]), 0.0, below)
        values = jnp.concatenate([above[None], inner, below[None]], axis=0)
        main = values[..., :MAIN].astype(BF16)
        rest = tails(values)
        return side_by_side(
            [main[a : a + SH] for a in range(3)], [rest[a : a + SH] for a in range(3)]
        ).reshape(cells, 4 * MAIN)

    def multiply(index, wide):
        return [
            jnp.dot(
                wide,
                weights[index][:, part * MAIN : (part + 1) * MAIN],
                preferred_element_type=F32,
            )
            for part in range(4)
        ]

    def collect(index, strip, products):
        early, same, late, rest = products
        low, high = slice(0, MAIN), slice(MAIN, MAIN + LANES)
        main = moved(index, 0, strip, early, low) + same + moved(index, 1, strip, late, low)
        ends = (
            moved(index, 0, strip, rest[:, :LANES], high)
            + pltpu.roll(rest[:, :LANES], LANES // 2, 1)
            + moved(index, 1, strip, rest[:, LANES:], high)
        )
        return jnp.concatenate([main, ends[:, : channels - MAIN]], axis=1)

    def straight(places, others):
        fresh = {}

        def span_of(place):
            return pl.ds(places[place] * SH, SH)

        def begin(index, place):
            if index == 0:
                inner = act(tile[span_of(place)].astype(F32), *stats[0])
            else:
                inner = act(fresh[place].astype(F32), *stats[1])
            return multiply(index, windows(index, places[place], inner))

        def finish(index, place, products):
            span, live = span_of(place), refresh[0, places[place]] > 0
            summed = collect(index, places[place], products)
            if index == 0:
                value = (summed + shift[...].reshape(1, channels)).astype(BF16)
                fresh[place] = value.reshape(SH, tile_cols, channels)
                hidden[span] = jnp.where(live, fresh[place], stale_hid[span])
                made, out = hidden, hidden_out
            else:
                value = tile[span].astype(F32) + summed.reshape(SH, tile_cols, channels)
                finished[span] = jnp.where(live, value.astype(BF16), tile[span])
                made, out = finished, block_out
            pltpu.make_async_copy(made.at[span], out.at[span], store_sem.at[index]).start()

        loads[0].wait()
        margin_terms(0)
        waiting, waited = [], False
        for start in range(0, len(places), AHEAD):
            for index in range(2):
                for place in range(start, min(start + AHEAD, len(places))):
                    waiting.append((index, place, begin(index, place)))
                    if len(waiting) < 2:
                        continue
                    if not waited:
                        for copy in loads[1:]:
                            copy.wait()
                        margin_terms(1)
                        for strip in others:
                            span = pl.ds(strip * SH, SH)
                            pltpu.make_async_copy(
                                stale_hid.at[span], hidden_out.at[span], store_sem.at[0]
                            ).start()
                            pltpu.make_async_copy(
                                tile.at[span], block_out.at[span], store_sem.at[1]
                            ).start()
                        waited = True
                    finish(*waiting.pop(0))
        finish(*waiting.pop(0))

    for count in range(1, strips // 2 + 1):

        @pl.when(pairs == count)
        def _():
            if 2 * count == strips:
                listed = list(range(strips))
            else:
                listed = [order[place] for place in range(strips)]
            straight(listed[: 2 * count], listed[2 * count :])

    total_wait(hidden, store_sem.at[0])
    total_wait(finished, store_sem.at[1])


def refreshed(
    shape,
    refresh,
    totals,
    gain_one,
    gain_two,
    rows,
    cols,
    shift,
    tile,
    first_weights,
    second_weights,
    stale_hid,
):
    tile_shape = tile.shape
    tile_rows, tile_cols, channels = tile_shape
    strip_total = tile_rows // SH
    anywhere = pl.BlockSpec(memory_space=pl.ANY)
    vmem = pl.BlockSpec(memory_space=pltpu.VMEM)
    out = jax.ShapeDtypeStruct(tile_shape, BF16)
    return pl.pallas_call(
        functools.partial(strips_kernel, shape),
        out_shape=(out, out),
        in_specs=[pl.BlockSpec(memory_space=pltpu.SMEM)] + [vmem] * 7 + [anywhere] * 3,
        out_specs=(anywhere, anywhere),
        scratch_shapes=[
            pltpu.VMEM((4 * MAIN, 4 * MAIN), BF16),
            pltpu.VMEM((4 * MAIN, 4 * MAIN), BF16),
            pltpu.VMEM(tile_shape, BF16),
            pltpu.SMEM((strip_total,), jnp.int32),
            pltpu.VMEM(cols.shape, F32),
            pltpu.VMEM((2, 2, tile_rows, MAIN + LANES), F32),
            pltpu.VMEM(tile_shape, BF16),
            pltpu.VMEM(tile_shape, BF16),
            pltpu.SemaphoreType.DMA((3,)),
            pltpu.SemaphoreType.DMA((2,)),
        ],
        compiler_params=pltpu.CompilerParams(vmem_limit_bytes=50 * 2**20),
        name="strips",
    )(
        refresh,
        totals,
        gain_one,
        gain_two,
        rows,
        cols,
        shift,
        tile,
        first_weights,
        second_weights,
        stale_hid,
    )


def per_device(
    shape,
    latent,
    stale_input,
    stale_hidden,
    refresh,
    gain_one,
    weight_one,
    time_shift,
    gain_two,
    weight_two,
):
    totals, rows, cols, tile, first_weights, second_weights = margins(
        shape, stale_input, stale_hidden, latent, weight_one, weight_two
    )
    return refreshed(
        shape,
        refresh.T,
        totals,
        gain_one,
        gain_two,
        rows,
        cols,
        time_shift,
        tile,
        first_weights,
        second_weights,
        stale_hidden,
    )


def solution(mesh):
    placed = (
        P("row", "col", None),
        P("row", "col", None),
        P("row", "col", None),
        P("row", "col"),
        P(),
        P(),
        P(),
        P(),
        P(),
    )
    return jax.shard_map(
        functools.partial(per_device, (mesh.shape["row"], mesh.shape["col"])),
        mesh=mesh,
        in_specs=placed,
        out_specs=(P("row", "col", None), P("row", "col", None)),
        check_vma=False,
    )
```
